256 devices in a mesh: mesh: 32 (over z_lo, y, core), tensor: 8 (over z_hi, x).
Axes of the slice: x: 4, y: 4, z: 8 (z_hi: 2, z_lo: 4; z = z_hi * 4 + z_lo), core: 2. Of those that a mesh axis runs over, the one named last changes fastest.
Arguments:
- cells: bfloat16 [65536, 1024], P('mesh'), may hold values from -10 to 10
- cotangent: bfloat16 [65536, 1024], P('mesh'), may hold values from -6 to 6
- counts: int32 [32], P('mesh'), may hold values from 1024 to 2048, as said below
- fx_weight: bfloat16 [1024, 1024], P(None, 'tensor'), may hold values from -0.1875 to 0.1875
- x_weight: bfloat16 [1024, 1024], P(None, 'tensor'), may hold values from -0.1875 to 0.1875
- slice_weight: bfloat16 [8, 128, 64], P('tensor'), may hold values from -0.5 to 0.5
- query_weight: float32 [8, 128, 128], P('tensor'), may hold values from -0.5 to 0.5
- key_weight: float32 [8, 128, 128], P('tensor'), may hold values from -0.5 to 0.5
- value_weight: float32 [8, 128, 128], P('tensor'), may hold values from -0.5 to 0.5
- out_weight: bfloat16 [1024, 1024], P('tensor'), may hold values from -0.1875 to 0.1875
Outputs:
- input_grad: bfloat16 [65536, 1024], P('mesh', 'tensor')
- fx_grad: float32 [1024, 1024], P(None, 'tensor')
- x_grad: float32 [1024, 1024], P(None, 'tensor')
- slice_grad: float32 [8, 128, 64], P('tensor')
- out_grad: float32 [1024, 1024], P('tensor')
The draws below stay inside these ranges and needn't reach their ends.
Inputs may be any that keep to these rules, and one draw needn't show every extreme that they name: Block b's live cells are its first counts[b] slots; in every draw some block is full.
All inputs are finite; a program needn't handle non-finite values.
Results may differ from the reference program's by a relative error of at most 0.03.
Values may be sent and summed in bfloat16 or wider, within the bound.
A program may use at most 64 MiB of HBM per device.

```python
import jax
import jax.numpy as jnp
from jax import lax

WIDTH = 1024
HEADS = 8
HEAD_DIM = 128
SLICES = 64
CELLS_DEV = 2048
BLOCKS = 32
CELLS = 65536
INNER = 1024


def draw_counts(key, part):
    key = jax.random.fold_in(key, 7)
    first, second = jax.random.split(key)
    counts = jax.random.randint(first, (BLOCKS,), CELLS_DEV // 2, CELLS_DEV + 1)
    full = jax.random.randint(second, (), 0, BLOCKS)
    return jnp.where(jnp.arange(BLOCKS) == full, CELLS_DEV, counts).astype(jnp.int32)


def draw_cells(key, part):
    key = jax.random.fold_in(key, 11)
    pick_key, centre_key, noise_key = jax.random.split(key, 3)
    block = jnp.arange(CELLS, dtype=jnp.int32) // CELLS_DEV
    spread = max(SLICES // 4, 2)
    state = (block * 5 + jax.random.randint(pick_key, (CELLS,), 0, spread)) % SLICES
    centres = 2.0 * jax.random.normal(centre_key, (SLICES, WIDTH), jnp.float32)
    centres = jnp.clip(centres, -6.0, 6.0)
    noise = jnp.clip(jax.random.normal(noise_key, (CELLS, WIDTH), jnp.float32), -4.0, 4.0)
    return (noise + jnp.take(centres, state, axis=0)).astype(jnp.bfloat16)


def shard_levels(own_key, dims, shards, smallest, high):
    def one(dim, blocks):
        heights = jax.random.uniform(jax.random.fold_in(jax.random.fold_in(own_key, 6), dim), (blocks,), jnp.float32, smallest / len(shards), high / len(shards))
        return jnp.repeat(jnp.exp(heights), dims[dim] // blocks).reshape((-1,) + (1,) * (len(dims) - dim - 1))

    gain = one(*shards[0])
    for cut in shards[1:]:
        gain = gain * one(*cut)
    return gain


def bell_draw(rng, shape, deviation, reach, cuts=(), held_as=jnp.bfloat16):
    values = jax.random.normal(rng, shape, jnp.float32) * deviation
    if len(cuts) > 0:
        values = shard_levels(rng, shape, cuts, -0.22, 0.18) * values
    return jnp.clip(values, min=-reach, max=reach).astype(held_as)


def setup_inputs(seed: int = 0) -> dict:
    streams_of = jax.random.split(jax.random.key(seed), 11)
    return {
        "cells": draw_cells(jax.random.fold_in(streams_of[10], 71), 0),
        "cotangent": bell_draw(streams_of[1], (CELLS, WIDTH), 1.0, 6.0, ((0, 32),)),
        "counts": draw_counts(jax.random.fold_in(streams_of[10], 71), 0),
        "fx_weight": bell_draw(streams_of[3], (WIDTH, INNER), WIDTH ** -0.5, 0.1875, ((1, 8),)),
        "x_weight": bell_draw(streams_of[4], (WIDTH, INNER), WIDTH ** -0.5, 0.1875, ((1, 8),)),
        "slice_weight": bell_draw(streams_of[5], (HEADS, HEAD_DIM, SLICES), HEAD_DIM ** -0.5, 0.5, ((0, 8),)),
        "query_weight": bell_draw(streams_of[6], (HEADS, HEAD_DIM, HEAD_DIM), HEAD_DIM ** -0.5, 0.5, ((0, 8),), jnp.float32),
        "key_weight": bell_draw(streams_of[7], (HEADS, HEAD_DIM, HEAD_DIM), HEAD_DIM ** -0.5, 0.5, ((0, 8),), jnp.float32),
        "value_weight": bell_draw(streams_of[8], (HEADS, HEAD_DIM, HEAD_DIM), HEAD_DIM ** -0.5, 0.5, ((0, 8),), jnp.float32),
        "out_weight": bell_draw(streams_of[9], (INNER, WIDTH), INNER ** -0.5, 0.1875, ((0, 8),)),
    }


def attend(tokens, query_weight, key_weight, value_weight):
    hp = lax.Precision.HIGHEST
    query = jnp.einsum('hgd,hde->hge', tokens, query_weight, precision=hp)
    keys = jnp.einsum('hgd,hde->hge', tokens, key_weight, precision=hp)
    values = jnp.einsum('hgd,hde->hge', tokens, value_weight, precision=hp)
    scores = jnp.einsum('hge,hke->hgk', query, keys, precision=hp) / jnp.sqrt(jnp.float32(query.shape[-1]))
    probs = jax.nn.softmax(scores, axis=-1)
    return jnp.einsum('hgk,hke->hge', probs, values, precision=hp)

def reference(cells, cotangent, counts, fx_weight, x_weight, slice_weight, query_weight, key_weight, value_weight, out_weight):
    f32 = jnp.float32
    slots = lax.iota(jnp.int32, CELLS)
    limit = jnp.repeat(counts.astype(jnp.int32), CELLS_DEV)
    live = (slots % CELLS_DEV < limit).astype(f32)
    feats = jnp.dot(cells, fx_weight, preferred_element_type=f32).astype(jnp.bfloat16)
    mixed = jnp.dot(cells, x_weight, preferred_element_type=f32).astype(jnp.bfloat16)
    feats3 = feats.reshape(CELLS, HEADS, HEAD_DIM).astype(f32)
    mixed3 = mixed.reshape(CELLS, HEADS, HEAD_DIM).astype(f32)
    slicer = slice_weight.astype(f32)
    logits = jnp.einsum('nhd,hdg->nhg', mixed3, slicer)
    slice_prob = jax.nn.softmax(logits, axis=-1) * live[:, None, None]
    prob_b = slice_prob.astype(jnp.bfloat16).astype(f32)
    sums = jnp.einsum('nhg,nhd->hgd', prob_b, feats3)
    totals = lax.optimization_barrier(jnp.sum(slice_prob, axis=0))
    denom = totals + 1e-05
    tokens = sums / denom[:, :, None]
    attended, attend_back = jax.vjp(attend, tokens, query_weight, key_weight, value_weight)
    attended_b = attended.astype(jnp.bfloat16).astype(f32)
    outputs = jnp.einsum('nhg,hgd->nhd', prob_b, attended_b).astype(jnp.bfloat16).reshape(CELLS, INNER)
    upstream = lax.dot_general(cotangent, out_weight, (((1,), (1,)), ((), ())), preferred_element_type=f32).astype(jnp.bfloat16)
    out_grad = lax.dot_general(outputs, cotangent, (((0,), (0,)), ((), ())), preferred_element_type=f32)
    upstream3 = upstream.reshape(CELLS, HEADS, HEAD_DIM).astype(f32)
    grad_attended = jnp.einsum('nhg,nhd->hgd', prob_b, upstream3)
    grad_tokens = attend_back(grad_attended)[0]
    grad_sums = (grad_tokens / denom[:, :, None]).astype(jnp.bfloat16).astype(f32)
    grad_totals = -lax.optimization_barrier(jnp.sum(grad_tokens * tokens, axis=-1)) / denom
    grad_prob = jnp.einsum('nhd,hgd->nhg', upstream3, attended_b) + jnp.einsum('nhd,hgd->nhg', feats3, grad_sums) + grad_totals[None]
    grad_feats = jnp.einsum('nhg,hgd->nhd', prob_b, grad_sums).astype(jnp.bfloat16)
    grad_logits = (slice_prob * (grad_prob - lax.optimization_barrier(jnp.sum(slice_prob * grad_prob, axis=-1, keepdims=True)))).astype(jnp.bfloat16)
    grad_logits32 = grad_logits.astype(f32)
    grad_mixed = jnp.einsum('nhg,hdg->nhd', grad_logits32, slicer).astype(jnp.bfloat16)
    slice_grad = jnp.einsum('nhd,nhg->hdg', mixed3, grad_logits32)
    grad_feats2 = grad_feats.reshape(CELLS, INNER)
    grad_mixed2 = grad_mixed.reshape(CELLS, INNER)
    contract = (((0,), (0,)), ((), ()))
    fx_grad = lax.dot_general(cells, grad_feats2, contract, preferred_element_type=f32)
    x_grad = lax.dot_general(cells, grad_mixed2, contract, preferred_element_type=f32)
    back = (((1,), (1,)), ((), ()))
    input_grad = lax.dot_general(grad_feats2, fx_weight, back, preferred_element_type=f32) + lax.dot_general(grad_mixed2, x_weight, back, preferred_element_type=f32)
    return (input_grad.astype(jnp.bfloat16), fx_grad, x_grad, slice_grad, out_grad)
```

```python
import jax
import jax.numpy as jnp
from jax import lax
from jax.experimental import pallas as pl
from jax.experimental.pallas import tpu as pltpu
from jax.sharding import PartitionSpec as P

MESH = pl.DeviceIdType.MESH
F32 = jnp.float32
BF16 = jnp.bfloat16
ROWS = 2048
WIDTH = 1024
DIM = 128
SL = 64
CHUNK = 512
NCHUNK = ROWS // CHUNK
PEERS = [(dy, dc) for dy in range(4) for dc in range(2) if dy or dc]
NT = (((1,), (1,)), ((), ()))


def dot(a, b):
    return jnp.dot(a, b, preferred_element_type=F32)


def dot_nt(a, b):
    return lax.dot_general(a, b, NT, preferred_element_type=F32)


def precise(a, b):
    return jnp.dot(a, b, preferred_element_type=F32, precision=lax.Precision.HIGHEST)


def precise_nt(a, b):
    return lax.dot_general(
        a, b, NT, preferred_element_type=F32, precision=lax.Precision.HIGHEST
    )


class Place:
    def __init__(self):
        m = lax.axis_index("mesh")
        t = lax.axis_index("tensor")
        self.zl, self.y, self.c = lax.div(m, 8), lax.rem(lax.div(m, 2), 4), lax.rem(m, 2)
        self.zh, self.x, self.t = lax.div(t, 4), lax.rem(t, 4), t
        self.m = m
        self.g = self.y * 2 + self.c
        x, c = self.x, self.c
        self.xp = (1 - c) * (x + 1 - 2 * lax.rem(x, 2)) + c * (3 - x)
        self.xq = c * (x + 1 - 2 * lax.rem(x, 2)) + (1 - c) * (3 - x)
        self.zp = 1 - self.zh
        self.tq = self.zh * 4 + self.xq

    def peer(self, dy, dc):
        yt, ct = lax.rem(self.y + dy, 4), lax.rem(self.c + dc, 2)
        yf = lax.rem(self.y + 4 - dy, 4)
        to = (self.zl * 8 + yt * 2 + ct, self.t)
        return to, yt * 2 + ct, yf * 2 + ct

    def plane(self, d):
        zt, zf = lax.rem(self.zl + d, 4), lax.rem(self.zl + 4 - d, 4)
        return (zt * 8 + self.g, self.t), zf

    def sibling(self):
        return (self.zl * 8 + self.y * 2 + 1 - self.c, self.t)

    def across(self, x_side, z_side):
        x = self.xp if x_side else self.x
        z = self.zp if z_side else self.zh
        return (self.m, z * 4 + x)

    def other_pair(self):
        return (self.m, self.tq)


class Sends:
    def __init__(self):
        self.all = []

    def start(self, src, dst, send_sem, recv_sem, device):
        copy = pltpu.make_async_remote_copy(
            src_ref=src,
            dst_ref=dst,
            send_sem=send_sem,
            recv_sem=recv_sem,
            device_id=device,
            device_id_type=MESH,
        )
        copy.start()
        self.all.append(copy)
        return copy

    def finish(self):
        for copy in self.all:
            copy.wait_send()


class AllReduce:
    def __init__(self, place, sends, src, rbuf, zbuf, full, ss, rs):
        self.p, self.sends = place, sends
        self.src, self.rbuf, self.zbuf, self.full = src, rbuf, zbuf, full
        self.ss, self.rs = ss, rs

    def arrived(self, dst, i):
        pltpu.make_async_remote_copy(
            src_ref=dst,
            dst_ref=dst,
            send_sem=self.ss.at[i],
            recv_sem=self.rs.at[i],
            device_id=self.p.sibling(),
            device_id_type=MESH,
        ).wait_recv()

    def step1(self):
        for i, (dy, dc) in enumerate(PEERS):
            to, j, _ = self.p.peer(dy, dc)
            self.sends.start(self.src.at[j], self.rbuf.at[i], self.ss.at[i], self.rs.at[i], to)

    def step2(self):
        for i in range(7):
            self.arrived(self.rbuf.at[i], i)
        total = self.src[self.p.g].astype(F32)
        for i in range(7):
            total += self.rbuf[i].astype(F32)
        zl = self.p.zl
        self.zbuf[zl] = total.astype(self.zbuf.dtype)
        for d in range(1, 4):
            to, _ = self.p.plane(d)
            i = 6 + d
            self.sends.start(self.zbuf.at[zl], self.zbuf.at[zl], self.ss.at[i], self.rs.at[i], to)

    def step3(self):
        for d in range(1, 4):
            _, zf = self.p.plane(d)
            self.arrived(self.zbuf.at[zf], 6 + d)
        total = self.zbuf[0].astype(F32)
        for i in range(1, 4):
            total += self.zbuf[i].astype(F32)
        g = self.p.g
        self.full[g] = total.astype(self.full.dtype)
        for i, (dy, dc) in enumerate(PEERS):
            to, _, _ = self.p.peer(dy, dc)
            k = 10 + i
            self.sends.start(self.full.at[g], self.full.at[g], self.ss.at[k], self.rs.at[k], to)

    def step4(self):
        for i, (dy, dc) in enumerate(PEERS):
            _, _, j = self.p.peer(dy, dc)
            self.arrived(self.full.at[j], 10 + i)


def attention(ar_full, w3, tok_w):
    flat = ar_full[...].reshape(SL, 384)
    totals = jnp.sum(flat[:, 256:384], axis=1, keepdims=True)
    denom = totals + 1e-05
    tokens = flat[:, 0:128] / denom
    d_out = flat[:, 128:256]
    scale = 1.0 / (DIM**0.5)
    qkv = precise(tokens, w3[...])
    q, k, v = qkv[:, 0:128], qkv[:, 128:256], qkv[:, 256:384]
    s = precise_nt(q, k) * scale
    st = precise_nt(k, q) * scale
    dp = precise_nt(d_out, v)
    dpt = precise_nt(v, d_out)
    e = jnp.exp(s - jnp.max(s, axis=1, keepdims=True))
    p = e / jnp.sum(e, axis=1, keepdims=True)
    et = jnp.exp(st - jnp.max(st, axis=0, keepdims=True))
    pt = et / jnp.sum(et, axis=0, keepdims=True)
    attended = precise(p, v)
    ds = p * (dp - jnp.sum(p * dp, axis=1, keepdims=True)) * scale
    dst = pt * (dpt - jnp.sum(pt * dpt, axis=0, keepdims=True)) * scale
    dv = precise(pt, d_out)
    dq = precise(ds, k)
    dk = precise(dst, q)
    tok_w[:, 0:128] = dq
    tok_w[:, 128:256] = dk
    tok_w[:, 256:384] = dv
    grad_tokens = precise_nt(tok_w[...], w3[...])
    grad_sums = (grad_tokens / denom).astype(BF16)
    prod = grad_tokens * tokens
    col = -jnp.sum(prod, axis=1, keepdims=True) / denom
    return attended.astype(BF16), grad_sums, col


def main_kernel(
    cells_h, cot_h, counts, fx_h, xw_h, sw_h, qw_h, kw_h, vw_h, ow_h,
    out_h, px_h, pg_h, ag_h, swt_h,
    cells, cot, wa, wo, swt, sw, w3, fu, pf, st, xs, xr, outb, mt, tokw,
    acc, accb, ag, gt,
    a1r, a1z, a1f, a2s, a2r, a2z, a2f, a3s, a3r, a3z, a3f,
    lsem, csem, tsem, osem, wss, wrs, gss, grs, xss, xrs,
    s1, r1, s2, r2, s3, r3,
):
    p = Place()
    sends = Sends()
    local = []

    def load(src, dst, sem):
        copy = pltpu.make_async_copy(src, dst, sem)
        copy.start()
        return copy

    l_xw = load(xw_h, wa.at[0, :, 0:128], lsem.at[0])
    l_fx = load(fx_h, wa.at[0, :, 128:256], lsem.at[1])
    l_sw = load(sw_h.at[0], sw, lsem.at[2])
    l_ow = load(ow_h, wo.at[0], lsem.at[3])
    l_cells, l_cot = [], []
    for r in range(NCHUNK):
        rows = pl.ds(r * CHUNK, CHUNK)
        l_cells.append(load(cells_h.at[rows], cells.at[rows], csem.at[r]))
        l_cot.append(load(cot_h.at[rows], cot.at[rows], tsem.at[r]))
    l_q = load(qw_h.at[0], w3.at[:, 0:128], lsem.at[4])
    l_k = load(kw_h.at[0], w3.at[:, 128:256], lsem.at[5])
    l_v = load(vw_h.at[0], w3.at[:, 256:384], lsem.at[6])

    barrier = pltpu.get_barrier_semaphore()
    friends = [p.peer(dy, dc)[0] for dy, dc in PEERS]
    friends += [p.plane(d)[0] for d in range(1, 4)]
    friends += [p.across(0, 1), p.across(1, 0), p.across(1, 1), p.other_pair()]
    for device in friends:
        pl.semaphore_signal(barrier, inc=1, device_id=device, device_id_type=MESH)
    pl.semaphore_wait(barrier, len(friends))

    c = p.c

    def part(i, half):
        if i < 2:
            start = pl.multiple_of(half * 512 + i * 256, 256)
            return lambda slot: wa.at[slot, pl.ds(start, 256), :]
        start = pl.multiple_of(half * 64, 64)
        return lambda slot: wo.at[slot, pl.ds(start, 64), :]

    l_sw.wait()
    eye = (
        lax.broadcasted_iota(jnp.int32, (SL, SL), 0)
        == lax.broadcasted_iota(jnp.int32, (SL, SL), 1)
    )
    swt[0] = dot_nt(eye.astype(F32).astype(BF16), sw[...]).astype(BF16)
    l_xw.wait()
    l_fx.wait()
    sends.start(swt.at[0], swt.at[2], gss.at[0], grs.at[0], p.across(0, 1))
    for i in range(2):
        ref = part(i, c)
        sends.start(ref(0), ref(2), wss.at[i], wrs.at[i], p.across(0, 1))
    sends.start(swt.at[0], swt.at[1], gss.at[1], grs.at[1], p.across(1, 0))
    sends.start(wa.at[0], wa.at[1], wss.at[3], wrs.at[3], p.across(1, 0))
    l_ow.wait()
    ref = part(2, c)
    sends.start(ref(0), ref(2), wss.at[2], wrs.at[2], p.across(0, 1))
    sends.start(wo.at[0], wo.at[1], wss.at[4], wrs.at[4], p.across(1, 0))

    def arrived(dst, ssem, rsem):
        pltpu.make_async_remote_copy(
            src_ref=dst, dst_ref=dst, send_sem=ssem, recv_sem=rsem,
            device_id=p.sibling(), device_id_type=MESH,
        ).wait_recv()

    def forward_z(i):
        ref = part(i, c)
        arrived(ref(2), wss.at[i], wrs.at[i])
        sends.start(ref(2), ref(2), wss.at[5 + i], wrs.at[5 + i], p.sibling())
        sends.start(ref(2), ref(3), wss.at[8 + i], wrs.at[8 + i], p.across(1, 0))

    def forward_s(i):
        ref = part(i, 1 - c)
        arrived(ref(2), wss.at[5 + i], wrs.at[5 + i])
        sends.start(ref(2), ref(3), wss.at[11 + i], wrs.at[11 + i], p.across(1, 0))

    count = counts[0]

    def phase1(k):
        def body(r, _):
            rows = pl.ds(pl.multiple_of(r * CHUNK, CHUNK), CHUNK)
            if k == 0:
                pltpu.make_async_copy(cells_h.at[rows], cells.at[rows], csem.at[r]).wait()
            xf = dot(cells[rows, :], wa[k]).astype(BF16)
            fu[k, rows, 0:128] = xf[:, 128:256]
            logits = dot_nt(swt[k], xf[:, 0:128])
            e = jnp.exp(logits - jnp.max(logits, axis=0, keepdims=True))
            lane = lax.broadcasted_iota(jnp.int32, (1, CHUNK), 1) + r * CHUNK
            norm = jnp.where(lane < count, 1.0 / jnp.sum(e, axis=0, keepdims=True), 0.0)
            prob = e * norm
            prob_b = prob.astype(BF16)
            pf[k, :, rows] = prob
            st[k * 128 : k * 128 + 64, rows] = prob_b
            if k == 0:
                pltpu.make_async_copy(cot_h.at[rows], cot.at[rows], tsem.at[r]).wait()
            fu[k, rows, 128:256] = dot_nt(cot[rows, :], wo[k]).astype(BF16)
            if k == 0:
                acc[:, 0:256] += dot(prob_b, fu[0, rows, :])
                tot = acc[:, 256:384]
                for j in range(CHUNK // 128):
                    tot += prob[:, j * 128 : j * 128 + 128]
                acc[:, 256:384] = tot
            return 0

        lax.fori_loop(0, NCHUNK, body, 0)

    acc[...] = jnp.zeros_like(acc)
    phase1(0)
    accb[...] = acc[...].reshape(8, 8, 384)
    ar1 = AllReduce(p, sends, accb, a1r, a1z, a1f, s1, r1)
    ar1.step1()

    def products(lhs_row, rhs, dst, at):
        def body(j, _):
            cols = pl.ds(pl.multiple_of(j * 256, 256), 256)
            out = dot(st[lhs_row : lhs_row + 64, :], rhs[:, cols]).astype(BF16)
            dst[2 * j, :, at : at + 128] = out[:, 0:128]
            dst[2 * j + 1, :, at : at + 128] = out[:, 128:256]
            return 0

        lax.fori_loop(0, 4, body, 0)

    products(0, cells, a2s, 0)
    ar1.step2()
    products(0, cot, a2s, 128)
    ar2 = AllReduce(p, sends, a2s, a2r, a2z, a2f, s2, r2)
    ar1.step3()
    ar2.step1()

    arrived(swt.at[1], gss.at[1], grs.at[1])
    arrived(wa.at[1], wss.at[3], wrs.at[3])
    arrived(wo.at[1], wss.at[4], wrs.at[4])
    phase1(1)
    arrived(swt.at[2], gss.at[0], grs.at[0])
    sends.start(swt.at[2], swt.at[3], gss.at[2], grs.at[2], p.across(1, 0))
    forward_z(0)
    l_q.wait()
    l_k.wait()
    l_v.wait()
    ar1.step4()
    att, gsum, col0 = attention(a1f, w3, tokw)
    ag[0, :, 0:128] = gsum
    ag[0, :, 128:256] = att
    gt[0] = jnp.broadcast_to(jnp.sum(jnp.where(eye, col0, 0.0), axis=0, keepdims=True), (8, SL))
    for slot, device in ((1, p.across(1, 0)), (2, p.across(0, 1)), (3, p.across(1, 1))):
        i = 1 + 2 * slot
        sends.start(ag.at[0], ag.at[slot], gss.at[i], grs.at[i], device)
        sends.start(gt.at[0], gt.at[slot], gss.at[i + 1], grs.at[i + 1], device)
    forward_s(0)
    forward_z(1)
    ar2.step2()

    def phase3(k):
        row = gt[k][0:1, :]
        col = jnp.sum(jnp.where(eye, row, 0.0), axis=1, keepdims=True)

        def body(r, _):
            rows = pl.ds(pl.multiple_of(r * CHUNK, CHUNK), CHUNK)
            gp = dot_nt(ag[k], fu[k, rows, :]) + col
            prob = pf[k, :, rows]
            mean = jnp.sum(prob * gp, axis=0, keepdims=True)
            st[k * 128 + 64 : k * 128 + 128, rows] = (prob * (gp - mean)).astype(BF16)
            return 0

        lax.fori_loop(0, NCHUNK, body, 0)

    phase3(0)
    products(64, cells, a3s, 0)
    ar3 = AllReduce(p, sends, a3s, a3r, a3z, a3f, s3, r3)
    ar3.step1()
    forward_s(1)
    forward_z(2)
    ar2.step3()
    forward_s(2)
    ar3.step2()
    phase1(2)
    ar3.step3()
    arrived(swt.at[3], gss.at[2], grs.at[2])
    for i in range(3):
        arrived(part(i, c)(3), wss.at[8 + i], wrs.at[8 + i])
        arrived(part(i, 1 - c)(3), wss.at[11 + i], wrs.at[11 + i])
    phase1(3)
    for slot in (1, 2, 3):
        i = 1 + 2 * slot
        arrived(ag.at[slot], gss.at[i], grs.at[i])
        arrived(gt.at[slot], gss.at[i + 1], grs.at[i + 1])
        phase3(slot)

    def columns(slot, t):
        rows = pl.ds(pl.multiple_of(t * 128, 128), 128)
        for k in range(4):
            mt[slot, :, k * 128 : k * 128 + 64] = dot_nt(
                wa[k, rows, 128:256], ag[k, :, 0:128]
            ).astype(BF16)
            mt[slot, :, k * 128 + 64 : k * 128 + 128] = dot_nt(
                wa[k, rows, 0:128], swt[k]
            ).astype(BF16)

    columns(0, p.tq)
    for r in range(NCHUNK):
        rows = pl.ds(r * CHUNK, CHUNK)
        xs[r] = dot(mt[0], st[:, rows]).astype(BF16)
        sends.start(xs.at[r], xr.at[r], xss.at[r], xrs.at[r], p.other_pair())
    columns(1, p.t)
    outs = []
    ar2.step4()
    outs.append(load(a2f, px_h, osem.at[0]))
    outs.append(load(ag.at[0], ag_h, osem.at[1]))
    outs.append(load(swt.at[0], swt_h, osem.at[2]))
    for r in range(NCHUNK):
        rows = pl.ds(r * CHUNK, CHUNK)
        own = dot(mt[1], st[:, rows])
        arrived(xr.at[r], xss.at[r], xrs.at[r])
        total = own + xr[r].astype(F32)
        outb[rows, :] = total.T.astype(BF16)
        outs.append(load(outb.at[rows], out_h.at[rows], osem.at[4 + r]))
    ar3.step4()
    outs.append(load(a3f, pg_h, osem.at[3]))
    for copy in outs:
        copy.wait()
    sends.finish()


def finish_kernel(out_in, px, pg, ag, swt, xw, out, fx_grad, x_grad, s_grad, o_grad, sem):
    copy = pltpu.make_async_copy(out_in, out, sem)
    copy.start()
    gs, att = ag[:, 0:128], ag[:, 128:256]
    att_t = att.astype(F32).T.astype(BF16)
    swt_v = swt[...]
    total = jnp.zeros((DIM, SL), F32)
    tn = (((0,), (0,)), ((), ()))
    for j in range(8):
        cols = slice(j * 128, j * 128 + 128)
        fx_grad[cols, :] = lax.dot_general(px[j, :, 0:128], gs, tn, preferred_element_type=F32)
        o_grad[:, cols] = dot(att_t, px[j, :, 128:256])
        x_grad[cols, :] = lax.dot_general(pg[j], swt_v, tn, preferred_element_type=F32)
        total += lax.dot_general(
            xw[cols, :], pg[j], (((0,), (1,)), ((), ())), preferred_element_type=F32
        )
    s_grad[0] = total
    copy.wait()


def shards(cells, cot, counts, fx_w, x_w, s_w, q_w, k_w, v_w, o_w):
    hbm = pl.BlockSpec(memory_space=pl.ANY)
    vmem = pl.BlockSpec(memory_space=pltpu.VMEM)
    sds = jax.ShapeDtypeStruct
    dma = pltpu.SemaphoreType.DMA
    V = pltpu.VMEM
    out_t, px, pg, ag, swt = pl.pallas_call(
        main_kernel,
        name="layer",
        out_shape=(
            sds((ROWS, DIM), BF16),
            sds((8, SL, 256), BF16),
            sds((8, SL, 128), BF16),
            sds((SL, 256), BF16),
            sds((SL, 128), BF16),
        ),
        in_specs=[hbm, hbm, pl.BlockSpec(memory_space=pltpu.SMEM)] + [hbm] * 7,
        out_specs=[hbm] * 5,
        scratch_shapes=[
            V((ROWS, WIDTH), BF16),
            V((ROWS, WIDTH), BF16),
            V((4, WIDTH, 256), BF16),
            V((4, DIM, WIDTH), BF16),
            V((4, SL, 128), BF16),
            V((DIM, SL), BF16),
            V((DIM, 384), F32),
            V((4, ROWS, 256), BF16),
            V((4, SL, ROWS), F32),
            V((512, ROWS), BF16),
            V((NCHUNK, DIM, CHUNK), BF16),
            V((NCHUNK, DIM, CHUNK), BF16),
            V((ROWS, DIM), BF16),
            V((2, DIM, 512), BF16),
            V((SL, 384), F32),
            V((SL, 384), F32),
            V((8, 8, 384), F32),
            V((4, SL, 256), BF16),
            V((4, 8, SL), F32),
            V((7, 8, 384), F32),
            V((4, 8, 384), F32),
            V((8, 8, 384), F32),
            V((8, SL, 256), BF16),
            V((7, SL, 256), BF16),
            V((4, SL, 256), BF16),
            V((8, SL, 256), BF16),
            V((8, SL, 128), BF16),
            V((7, SL, 128), BF16),
            V((4, SL, 128), BF16),
            V((8, SL, 128), BF16),
            dma((7,)),
            dma((NCHUNK,)),
            dma((NCHUNK,)),
            dma((4 + NCHUNK,)),
            dma((14,)),
            dma((14,)),
            dma((9,)),
            dma((9,)),
            dma((NCHUNK,)),
            dma((NCHUNK,)),
        ]
        + [dma((17,))] * 6,
        compiler_params=pltpu.CompilerParams(
            collective_id=0, has_side_effects=True, vmem_limit_bytes=56 * 1024 * 1024
        ),
    )(cells, cot, counts, fx_w, x_w, s_w, q_w, k_w, v_w, o_w)
    return pl.pallas_call(
        finish_kernel,
        name="grads",
        out_shape=(
            sds((ROWS, DIM), BF16),
            sds((WIDTH, DIM), F32),
            sds((WIDTH, DIM), F32),
            sds((1, DIM, SL), F32),
            sds((DIM, WIDTH), F32),
        ),
        in_specs=[hbm] + [vmem] * 5,
        out_specs=[hbm] + [vmem] * 4,
        scratch_shapes=[dma],
        compiler_params=pltpu.CompilerParams(vmem_limit_bytes=32 * 1024 * 1024),
    )(out_t, px, pg, ag, swt, x_w)


def solution(mesh):
    in_specs = (
        P("mesh", None),
        P("mesh", None),
        P("mesh"),
        P(None, "tensor"),
        P(None, "tensor"),
        P("tensor", None, None),
        P("tensor", None, None),
        P("tensor", None, None),
        P("tensor", None, None),
        P("tensor", None),
    )
    out_specs = (
        P("mesh", "tensor"),
        P(None, "tensor"),
        P(None, "tensor"),
        P("tensor", None, None),
        P("tensor", None),
    )
    return jax.shard_map(shards, mesh=mesh, in_specs=in_specs, out_specs=out_specs, check_vma=False)
```

```python
import jax
import jax.numpy as jnp
from jax import lax
from jax.experimental import pallas as pl
from jax.experimental.pallas import tpu as pltpu
from jax.sharding import PartitionSpec as P

MESH = pl.DeviceIdType.MESH
F32 = jnp.float32
BF16 = jnp.bfloat16
ROWS = 2048
WIDTH = 1024
DIM = 128
SL = 64
CHUNK = 512
NCHUNK = ROWS // CHUNK
BIG = 1024
NBIG = ROWS // BIG
PEERS = [(dy, dc) for dy in range(4) for dc in range(2) if dy or dc]
NT = (((1,), (1,)), ((), ()))


def dot(a, b):
    return jnp.dot(a, b, preferred_element_type=F32)


def dot_nt(a, b):
    return lax.dot_general(a, b, NT, preferred_element_type=F32)


def precise(a, b):
    return jnp.dot(a, b, preferred_element_type=F32, precision=lax.Precision.HIGHEST)


def precise_nt(a, b):
    return lax.dot_general(
        a, b, NT, preferred_element_type=F32, precision=lax.Precision.HIGHEST
    )


class Place:
    def __init__(self):
        m = lax.axis_index("mesh")
        t = lax.axis_index("tensor")
        self.zl, self.y, self.c = lax.div(m, 8), lax.rem(lax.div(m, 2), 4), lax.rem(m, 2)
        self.zh, self.x, self.t = lax.div(t, 4), lax.rem(t, 4), t
        self.m = m
        self.g = self.y * 2 + self.c
        x, c = self.x, self.c
        self.xp = (1 - c) * (x + 1 - 2 * lax.rem(x, 2)) + c * (3 - x)
        self.xq = c * (x + 1 - 2 * lax.rem(x, 2)) + (1 - c) * (3 - x)
        self.zp = 1 - self.zh
        self.tq = self.zh * 4 + self.xq

    def peer(self, dy, dc):
        yt, ct = lax.rem(self.y + dy, 4), lax.rem(self.c + dc, 2)
        yf = lax.rem(self.y + 4 - dy, 4)
        to = (self.zl * 8 + yt * 2 + ct, self.t)
        return to, yt * 2 + ct, yf * 2 + ct

    def plane(self, d):
        zt, zf = lax.rem(self.zl + d, 4), lax.rem(self.zl + 4 - d, 4)
        return (zt * 8 + self.g, self.t), zf

    def sibling(self):
        return (self.zl * 8 + self.y * 2 + 1 - self.c, self.t)

    def across(self, x_side, z_side):
        x = self.xp if x_side else self.x
        z = self.zp if z_side else self.zh
        return (self.m, z * 4 + x)

    def other_pair(self):
        return (self.m, self.tq)


class Sends:
    def __init__(self):
        self.all = []

    def start(self, src, dst, send_sem, recv_sem, device):
        copy = pltpu.make_async_remote_copy(
            src_ref=src,
            dst_ref=dst,
            send_sem=send_sem,
            recv_sem=recv_sem,
            device_id=device,
            device_id_type=MESH,
        )
        copy.start()
        self.all.append(copy)
        return copy

    def finish(self):
        for copy in self.all:
            copy.wait_send()


class AllReduce:
    def __init__(self, place, sends, src, rbuf, zbuf, full, ss, rs):
        self.p, self.sends = place, sends
        self.src, self.rbuf, self.zbuf, self.full = src, rbuf, zbuf, full
        self.ss, self.rs = ss, rs

    def arrived(self, dst, i):
        pltpu.make_async_remote_copy(
            src_ref=dst,
            dst_ref=dst,
            send_sem=self.ss.at[i],
            recv_sem=self.rs.at[i],
            device_id=self.p.sibling(),
            device_id_type=MESH,
        ).wait_recv()

    def step1(self):
        for i, (dy, dc) in enumerate(PEERS):
            to, j, _ = self.p.peer(dy, dc)
            self.sends.start(self.src.at[j], self.rbuf.at[i], self.ss.at[i], self.rs.at[i], to)

    def step2(self):
        for i in range(7):
            self.arrived(self.rbuf.at[i], i)
        total = self.src[self.p.g].astype(F32)
        for i in range(7):
            total += self.rbuf[i].astype(F32)
        zl = self.p.zl
        self.zbuf[zl] = total.astype(self.zbuf.dtype)
        for d in range(1, 4):
            to, _ = self.p.plane(d)
            i = 6 + d
            self.sends.start(self.zbuf.at[zl], self.zbuf.at[zl], self.ss.at[i], self.rs.at[i], to)

    def step3(self):
        for d in range(1, 4):
            _, zf = self.p.plane(d)
            self.arrived(self.zbuf.at[zf], 6 + d)
        total = self.zbuf[0].astype(F32)
        for i in range(1, 4):
            total += self.zbuf[i].astype(F32)
        g = self.p.g
        self.full[g] = total.astype(self.full.dtype)
        for i, (dy, dc) in enumerate(PEERS):
            to, _, _ = self.p.peer(dy, dc)
            k = 10 + i
            self.sends.start(self.full.at[g], self.full.at[g], self.ss.at[k], self.rs.at[k], to)

    def step4(self):
        for i, (dy, dc) in enumerate(PEERS):
            _, _, j = self.p.peer(dy, dc)
            self.arrived(self.full.at[j], 10 + i)


def attention(ar_full, w3, tok_w):
    flat = ar_full[...].reshape(SL, 384)
    totals = jnp.sum(flat[:, 256:384], axis=1, keepdims=True)
    denom = totals + 1e-05
    tokens = flat[:, 0:128] / denom
    d_out = flat[:, 128:256]
    scale = 1.0 / (DIM**0.5)
    qkv = precise(tokens, w3[...])
    q, k, v = qkv[:, 0:128], qkv[:, 128:256], qkv[:, 256:384]
    s = precise_nt(q, k) * scale
    st = precise_nt(k, q) * scale
    dp = precise_nt(d_out, v)
    dpt = precise_nt(v, d_out)
    e = jnp.exp(s - jnp.max(s, axis=1, keepdims=True))
    p = e / jnp.sum(e, axis=1, keepdims=True)
    et = jnp.exp(st - jnp.max(st, axis=0, keepdims=True))
    pt = et / jnp.sum(et, axis=0, keepdims=True)
    attended = precise(p, v)
    ds = p * (dp - jnp.sum(p * dp, axis=1, keepdims=True)) * scale
    dst = pt * (dpt - jnp.sum(pt * dpt, axis=0, keepdims=True)) * scale
    dv = precise(pt, d_out)
    dq = precise(ds, k)
    dk = precise(dst, q)
    tok_w[:, 0:128] = dq
    tok_w[:, 128:256] = dk
    tok_w[:, 256:384] = dv
    grad_tokens = precise_nt(tok_w[...], w3[...])
    grad_sums = (grad_tokens / denom).astype(BF16)
    prod = grad_tokens * tokens
    col = -jnp.sum(prod, axis=1, keepdims=True) / denom
    return attended.astype(BF16), grad_sums, col


def main_kernel(
    cells_h, cot_h, counts, fx_h, xw_h, swt_h, qw_h, kw_h, vw_h, ow_h,
    out_h, px_h, pg_h, ag_h,
    cells, cot, w, wo, swt, w3, fu, pf, st, xs, xr, own, outb, mt, tokw,
    acc, accb, ag, gt, at1, at2,
    a1r, a1z, a1f, a2s, a2r, a2z, a2f, a3s, a3r, a3z, a3f,
    lsem, csem, tsem, osem, wss, wrs, gss, grs, xss, xrs,
    s1, r1, s2, r2, s3, r3,
):
    p = Place()
    sends = Sends()

    def load(src, dst, sem):
        copy = pltpu.make_async_copy(src, dst, sem)
        copy.start()
        return copy

    l_fx = load(fx_h, w.at[:, 0:128], lsem.at[0])
    l_xw = load(xw_h, w.at[:, 128:256], lsem.at[1])
    l_sw = load(swt_h.at[0], swt.at[0], lsem.at[2])
    l_ow = load(ow_h, wo.at[0], lsem.at[3])
    for r in range(NBIG):
        rows = pl.ds(r * BIG, BIG)
        load(cells_h.at[rows], cells.at[rows], csem.at[r])
        load(cot_h.at[rows], cot.at[rows], tsem.at[r])
    l_q = load(qw_h.at[0], w3.at[:, 0:128], lsem.at[4])
    l_k = load(kw_h.at[0], w3.at[:, 128:256], lsem.at[5])
    l_v = load(vw_h.at[0], w3.at[:, 256:384], lsem.at[6])

    barrier = pltpu.get_barrier_semaphore()
    friends = [p.peer(dy, dc)[0] for dy, dc in PEERS]
    friends += [p.plane(d)[0] for d in range(1, 4)]
    friends += [p.across(0, 1), p.across(1, 0), p.across(1, 1), p.other_pair()]
    for device in friends:
        pl.semaphore_signal(barrier, inc=1, device_id=device, device_id_type=MESH)
    pl.semaphore_wait(barrier, len(friends))

    c, y = p.c, p.y
    x_pair, z_pair = p.across(1, 0), p.across(0, 1)

    def start(i, src, dst, device):
        sends.start(src, dst, wss.at[i], wrs.at[i], device)

    def arrived(dst, ssem, rsem):
        pltpu.make_async_remote_copy(
            src_ref=dst, dst_ref=dst, send_sem=ssem, recv_sem=rsem,
            device_id=p.sibling(), device_id_type=MESH,
        ).wait_recv()

    def landed(i, dst):
        arrived(dst, wss.at[i], wrs.at[i])

    def w_part(core, quarter, lanes):
        rows = pl.ds(pl.multiple_of(core * 512 + quarter * 128, 128), 128)
        return w.at[rows, lanes]

    def w_half(core, lanes):
        return w.at[pl.ds(pl.multiple_of(core * 512, 512), 512), lanes]

    def wo_part(slot, core, quarter):
        return wo.at[slot, pl.ds(pl.multiple_of(core * 64 + quarter * 16, 16), 16), :]

    def wo_half(slot, core):
        return wo.at[slot, pl.ds(pl.multiple_of(core * 64, 64), 64), :]

    FX0, FX1, FX2 = slice(0, 256), slice(256, 512), slice(512, 768)
    F2, X2, X3, F3 = slice(512, 640), slice(640, 768), slice(768, 896), slice(896, 1024)

    l_fx.wait()
    l_xw.wait()
    start(0, w_part(c, y, FX0), w_part(c, y, FX2), z_pair)
    l_ow.wait()
    start(1, wo_part(0, c, y), wo_part(2, c, y), z_pair)
    l_sw.wait()
    sends.start(swt.at[0], swt.at[2], gss.at[0], grs.at[0], z_pair)
    start(2, w.at[:, FX0], w.at[:, FX1], x_pair)
    sends.start(swt.at[0], swt.at[1], gss.at[1], grs.at[1], x_pair)
    start(3, wo.at[0], wo.at[1], x_pair)

    def spread_w():
        landed(0, w_part(c, y, FX2))
        for d in range(1, 4):
            start(3 + d, w_part(c, y, FX2), w_part(c, y, FX2), p.peer(d, 0)[0])

    def spread_wo():
        landed(1, wo_part(2, c, y))
        for d in range(1, 4):
            start(6 + d, wo_part(2, c, y), wo_part(2, c, y), p.peer(d, 0)[0])

    def gather_w():
        for d in range(1, 4):
            landed(3 + d, w_part(c, lax.rem(y + 4 - d, 4), FX2))
        start(10, w_half(c, FX2), w_half(c, FX2), p.sibling())
        start(12, w_half(c, X2), w_half(c, X3), x_pair)

    def gather_wo():
        for d in range(1, 4):
            landed(6 + d, wo_part(2, c, lax.rem(y + 4 - d, 4)))
        start(11, wo_half(2, c), wo_half(2, c), p.sibling())

    def pass_on():
        landed(10, w_half(1 - c, FX2))
        start(13, w_half(1 - c, X2), w_half(1 - c, X3), x_pair)
        start(14, w_half(c, F2), w_half(c, F3), x_pair)
        start(15, wo_half(2, c), wo_half(3, c), x_pair)

    def pass_on_rest():
        landed(11, wo_half(2, 1 - c))
        start(16, w_half(1 - c, F2), w_half(1 - c, F3), x_pair)
        start(17, wo_half(2, 1 - c), wo_half(3, 1 - c), x_pair)

    count = counts[0]

    def big_rows(r):
        return pl.ds(pl.multiple_of(r * BIG, BIG), BIG)

    def softmax(k, r, mixed):
        rows = big_rows(r)
        logits = dot_nt(swt[k], mixed)
        e = jnp.exp(logits - jnp.max(logits, axis=0, keepdims=True))
        lane = lax.broadcasted_iota(jnp.int32, (1, BIG), 1) + r * BIG
        norm = jnp.where(lane < count, 1.0 / jnp.sum(e, axis=0, keepdims=True), 0.0)
        prob = e * norm
        pf[k, :, rows] = prob
        prob_b = prob.astype(BF16)
        st[k * 128 : k * 128 + 64, rows] = prob_b
        return prob, prob_b

    acc[...] = jnp.zeros_like(acc)

    def own_body(r, _):
        rows = big_rows(r)
        pltpu.make_async_copy(cells_h.at[rows], cells.at[rows], csem.at[r]).wait()
        xf = dot(cells[rows, :], w[:, FX0]).astype(BF16)
        fu[rows, 0:128] = xf[:, 0:128]
        prob, prob_b = softmax(0, r, xf[:, 128:256])
        pltpu.make_async_copy(cot_h.at[rows], cot.at[rows], tsem.at[r]).wait()
        fu[rows, 128:256] = dot_nt(cot[rows, :], wo[0]).astype(BF16)
        acc[:, 0:256] += dot(prob_b, fu[rows, :])
        tot = acc[:, 256:384]
        for j in range(BIG // 128):
            tot += prob[:, j * 128 : j * 128 + 128]
        acc[:, 256:384] = tot
        return 0

    lax.fori_loop(0, NBIG, own_body, 0)
    accb[...] = acc[...].reshape(8, 8, 384)
    ar1 = AllReduce(p, sends, accb, a1r, a1z, a1f, s1, r1)
    ar2 = AllReduce(p, sends, a2s, a2r, a2z, a2f, s2, r2)
    ar3 = AllReduce(p, sends, a3s, a3r, a3z, a3f, s3, r3)
    ar1.step1()

    def products(lhs_row, rhs, dst, at):
        def body(j, _):
            cols = pl.ds(pl.multiple_of(j * 512, 512), 512)
            out = dot(st[lhs_row : lhs_row + 64, :], rhs[:, cols]).astype(BF16)
            for i in range(4):
                dst[4 * j + i, :, at : at + 128] = out[:, i * 128 : i * 128 + 128]
            return 0

        lax.fori_loop(0, 2, body, 0)

    products(0, cells, a2s, 0)
    spread_w()
    products(0, cot, a2s, 128)
    spread_wo()
    ar1.step2()
    arrived(swt.at[2], gss.at[0], grs.at[0])
    sends.start(swt.at[2], swt.at[3], gss.at[2], grs.at[2], x_pair)
    arrived(swt.at[1], gss.at[1], grs.at[1])
    landed(2, w.at[:, FX1])

    def pair_body(r, _):
        mixed = dot(cells[big_rows(r), :], w[:, 384:512]).astype(BF16)
        softmax(1, r, mixed)
        return 0

    lax.fori_loop(0, NBIG, pair_body, 0)
    ar1.step3()
    gather_w()
    ar2.step1()
    gather_wo()
    landed(3, wo.at[1])
    pass_on()
    l_q.wait()
    l_k.wait()
    l_v.wait()
    ar1.step4()
    att, gsum, col0 = attention(a1f, w3, tokw)
    ag[0, :, 0:128] = gsum
    ag[0, :, 128:256] = att
    eye = (
        lax.broadcasted_iota(jnp.int32, (SL, SL), 0)
        == lax.broadcasted_iota(jnp.int32, (SL, SL), 1)
    )
    gt[0] = jnp.broadcast_to(jnp.sum(jnp.where(eye, col0, 0.0), axis=0, keepdims=True), (8, SL))
    for slot, device in ((3, p.across(1, 1)), (2, z_pair), (1, x_pair)):
        i = 1 + 2 * slot
        sends.start(ag.at[0], ag.at[slot], gss.at[i], grs.at[i], device)
        sends.start(gt.at[0], gt.at[slot], gss.at[i + 1], grs.at[i + 1], device)
    pass_on_rest()

    def vjp(k, rows, gp):
        prob = pf[k, :, rows]
        mean = jnp.sum(prob * gp, axis=0, keepdims=True)
        st[k * 128 + 64 : k * 128 + 128, rows] = (prob * (gp - mean)).astype(BF16)

    def own_vjp(r, _):
        rows = big_rows(r)
        vjp(0, rows, dot_nt(ag[0], fu[rows, :]) + col0)
        return 0

    lax.fori_loop(0, NBIG, own_vjp, 0)
    products(64, cells, a3s, 0)
    ar3.step1()
    ar2.step2()
    arrived(swt.at[3], gss.at[2], grs.at[2])
    landed(12, w_half(c, X3))
    landed(13, w_half(1 - c, X3))

    def far_body(r, _):
        mixed = dot(cells[big_rows(r), :], w[:, 640:896]).astype(BF16)
        softmax(2, r, mixed[:, 0:128])
        softmax(3, r, mixed[:, 128:256])
        return 0

    lax.fori_loop(0, NBIG, far_body, 0)
    ar2.step3()
    ar3.step2()

    f_at = (0, 256, 512, 896)
    x_at = (128, 384, 640, 768)
    col_rows = [pl.ds(pl.multiple_of(t * 128, 128), 128) for t in (p.tq, p.t)]

    def fixed_columns(k):
        for i, rows in enumerate(col_rows):
            mt[i, :, k * 128 + 64 : k * 128 + 128] = dot_nt(
                w[rows, x_at[k] : x_at[k] + 128], swt[k]
            ).astype(BF16)

    def sum_columns(k):
        for i, rows in enumerate(col_rows):
            mt[i, :, k * 128 : k * 128 + 64] = dot_nt(
                w[rows, f_at[k] : f_at[k] + 128], ag[k, :, 0:128]
            ).astype(BF16)

    def fold(k):
        i = 1 + 2 * k
        arrived(ag.at[k], gss.at[i], grs.at[i])
        arrived(gt.at[k], gss.at[i + 1], grs.at[i + 1])
        full = ag[k].astype(F32)
        centred = (full - jnp.mean(full, axis=0, keepdims=True)).astype(BF16)
        rows = slice((k - 1) * 64, k * 64)
        at1[rows, :] = dot_nt(centred[:, 0:128], w[:, f_at[k] : f_at[k] + 128]).astype(BF16)
        at2[rows, :] = dot(centred[:, 128:256], wo[k]).astype(BF16)
        sum_columns(k)

    for k in range(4):
        fixed_columns(k)
    sum_columns(0)
    fold(1)
    landed(14, w_half(c, F3))
    landed(15, wo_half(3, c))
    landed(16, w_half(1 - c, F3))
    landed(17, wo_half(3, 1 - c))
    fold(2)
    fold(3)
    gcol = [
        jnp.sum(jnp.where(eye, gt[k][0:1, :], 0.0), axis=1, keepdims=True) for k in (1, 2, 3)
    ]
    for r in range(NCHUNK):
        rows = pl.ds(r * CHUNK, CHUNK)
        gp = dot_nt(at1[...], cells[rows, :]) + dot_nt(at2[...], cot[rows, :])
        for k in (1, 2, 3):
            vjp(k, rows, gp[(k - 1) * 64 : k * 64, :] + gcol[k - 1])
        xs[r] = dot(mt[0], st[:, rows]).astype(BF16)
        sends.start(xs.at[r], xr.at[r], xss.at[r], xrs.at[r], p.other_pair())
    ar3.step3()
    outs = [load(ag.at[0], ag_h, osem.at[0])]
    ar2.step4()
    outs.append(load(a2f, px_h, osem.at[1]))
    for r in range(NCHUNK):
        rows = pl.ds(r * CHUNK, CHUNK)
        own[:, rows] = dot(mt[1], st[:, rows])
    for r in range(NCHUNK):
        rows = pl.ds(r * CHUNK, CHUNK)
        arrived(xr.at[r], xss.at[r], xrs.at[r])
        total = own[:, rows] + xr[r].astype(F32)
        outb[rows, :] = total.T.astype(BF16)
        outs.append(load(outb.at[rows], out_h.at[rows], osem.at[3 + r]))
    ar3.step4()
    outs.append(load(a3f, pg_h, osem.at[2]))
    for copy in outs:
        copy.wait()
    sends.finish()


def finish_kernel(
    out_in, px_h, pg_h, ag_h, swt_h, xw_h,
    out, fx_h, xg_h, sg_h, og_h,
    held, px, pg, ag, swt, xw, fx, xg, sg, og, sem,
):
    copies = []

    def move(src, dst, i):
        copy = pltpu.make_async_copy(src, dst, sem.at[i])
        copy.start()
        return copy

    l_px, l_ag = move(px_h, px, 0), move(ag_h, ag, 1)
    l_pg, l_swt, l_xw = move(pg_h, pg, 2), move(swt_h, swt, 3), move(xw_h, xw, 4)
    l_out = move(out_in, held, 5)
    l_px.wait()
    l_ag.wait()
    gs, att = ag[:, 0:128], ag[:, 128:256]
    att_t = att.astype(F32).T.astype(BF16)
    tn = (((0,), (0,)), ((), ()))
    for j in range(8):
        cols = slice(j * 128, j * 128 + 128)
        fx[cols, :] = lax.dot_general(px[j, :, 0:128], gs, tn, preferred_element_type=F32)
    copies.append(move(fx, fx_h, 6))
    l_out.wait()
    copies.append(move(held, out, 10))
    for j in range(8):
        cols = slice(j * 128, j * 128 + 128)
        og[:, cols] = dot(att_t, px[j, :, 128:256])
    copies.append(move(og, og_h, 7))
    l_pg.wait()
    l_swt.wait()
    swt_v = swt[0]
    for j in range(8):
        cols = slice(j * 128, j * 128 + 128)
        xg[cols, :] = lax.dot_general(pg[j], swt_v, tn, preferred_element_type=F32)
    copies.append(move(xg, xg_h, 8))
    l_xw.wait()
    total = jnp.zeros((SL, DIM), F32)
    for j in range(8):
        total += dot(pg[j], xw[j * 128 : j * 128 + 128, :])
    sg[0] = total
    copies.append(move(sg, sg_h, 9))
    for copy in copies:
        copy.wait()


def shards(cells, cot, counts, fx_w, x_w, s_w, q_w, k_w, v_w, o_w):
    hbm = pl.BlockSpec(memory_space=pl.ANY)
    sds = jax.ShapeDtypeStruct
    dma = pltpu.SemaphoreType.DMA
    V = pltpu.VMEM
    swt = jnp.swapaxes(s_w, 1, 2)
    limit = 60 * 1024 * 1024
    out, px, pg, ag = pl.pallas_call(
        main_kernel,
        name="layer",
        out_shape=(
            sds((ROWS, DIM), BF16),
            sds((8, SL, 256), BF16),
            sds((8, SL, 128), BF16),
            sds((SL, 256), BF16),
        ),
        in_specs=[hbm, hbm, pl.BlockSpec(memory_space=pltpu.SMEM)] + [hbm] * 7,
        out_specs=[hbm] * 4,
        scratch_shapes=[
            V((ROWS, WIDTH), BF16),
            V((ROWS, WIDTH), BF16),
            V((WIDTH, 1024), BF16),
            V((4, DIM, WIDTH), BF16),
            V((4, SL, 128), BF16),
            V((DIM, 384), F32),
            V((ROWS, 256), BF16),
            V((4, SL, ROWS), F32),
            V((512, ROWS), BF16),
            V((NCHUNK, DIM, CHUNK), BF16),
            V((NCHUNK, DIM, CHUNK), BF16),
            V((DIM, ROWS), F32),
            V((ROWS, DIM), BF16),
            V((2, DIM, 512), BF16),
            V((SL, 384), F32),
            V((SL, 384), F32),
            V((8, 8, 384), F32),
            V((4, SL, 256), BF16),
            V((4, 8, SL), F32),
            V((192, WIDTH), BF16),
            V((192, WIDTH), BF16),
            V((7, 8, 384), F32),
            V((4, 8, 384), F32),
            V((8, 8, 384), F32),
            V((8, SL, 256), BF16),
            V((7, SL, 256), BF16),
            V((4, SL, 256), BF16),
            V((8, SL, 256), BF16),
            V((8, SL, 128), BF16),
            V((7, SL, 128), BF16),
            V((4, SL, 128), BF16),
            V((8, SL, 128), BF16),
            dma((7,)),
            dma((NBIG,)),
            dma((NBIG,)),
            dma((3 + NCHUNK,)),
            dma((18,)),
            dma((18,)),
            dma((9,)),
            dma((9,)),
            dma((NCHUNK,)),
            dma((NCHUNK,)),
        ]
        + [dma((17,))] * 6,
        compiler_params=pltpu.CompilerParams(
            collective_id=0, has_side_effects=True, vmem_limit_bytes=limit
        ),
    )(cells, cot, counts, fx_w, x_w, swt, q_w, k_w, v_w, o_w)
    outs = pl.pallas_call(
        finish_kernel,
        name="grads",
        out_shape=(
            sds((ROWS, DIM), BF16),
            sds((WIDTH, DIM), F32),
            sds((WIDTH, DIM), F32),
            sds((1, SL, DIM), F32),
            sds((DIM, WIDTH), F32),
        ),
        in_specs=[hbm] * 6,
        out_specs=[hbm] * 5,
        scratch_shapes=[
            V((ROWS, DIM), BF16),
            V((8, SL, 256), BF16),
            V((8, SL, 128), BF16),
            V((SL, 256), BF16),
            V((1, SL, 128), BF16),
            V((WIDTH, DIM), BF16),
            V((WIDTH, DIM), F32),
            V((WIDTH, DIM), F32),
            V((1, SL, DIM), F32),
            V((DIM, WIDTH), F32),
            dma((11,)),
        ],
        compiler_params=pltpu.CompilerParams(vmem_limit_bytes=limit),
    )(out, px, pg, ag, swt, x_w)
    return outs[0], outs[1], outs[2], jnp.swapaxes(outs[3], 1, 2), outs[4]


def solution(mesh):
    in_specs = (
        P("mesh", None),
        P("mesh", None),
        P("mesh"),
        P(None, "tensor"),
        P(None, "tensor"),
        P("tensor", None, None),
        P("tensor", None, None),
        P("tensor", None, None),
        P("tensor", None, None),
        P("tensor", None),
    )
    out_specs = (
        P("mesh", "tensor"),
        P(None, "tensor"),
        P(None, "tensor"),
        P("tensor", None, None),
        P("tensor", None),
    )
    return jax.shard_map(shards, mesh=mesh, in_specs=in_specs, out_specs=out_specs, check_vma=False)
```

```python
import jax
import jax.numpy as jnp
from jax import lax
from jax.experimental import pallas as pl
from jax.experimental.pallas import tpu as pltpu
from jax.sharding import PartitionSpec as P

MESH = pl.DeviceIdType.MESH
F32 = jnp.float32
BF16 = jnp.bfloat16
ROWS = 2048
WIDTH = 1024
DIM = 128
SL = 64
CHUNK = 512
NCHUNK = ROWS // CHUNK
EDGES = (0, 512, 1024, 1536, 2048)
NLATE = len(EDGES) - 1
BIG = 1024
NBIG = ROWS // BIG
PEERS = [(dy, dc) for dy in range(4) for dc in range(2) if dy or dc]
NT = (((1,), (1,)), ((), ()))


def dot(a, b):
    return jnp.dot(a, b, preferred_element_type=F32)


def dot_nt(a, b):
    return lax.dot_general(a, b, NT, preferred_element_type=F32)


def precise(a, b):
    return jnp.dot(a, b, preferred_element_type=F32, precision=lax.Precision.HIGHEST)


def precise_nt(a, b):
    return lax.dot_general(
        a, b, NT, preferred_element_type=F32, precision=lax.Precision.HIGHEST
    )


class Place:
    def __init__(self):
        m = lax.axis_index("mesh")
        t = lax.axis_index("tensor")
        self.zl, self.y, self.c = lax.div(m, 8), lax.rem(lax.div(m, 2), 4), lax.rem(m, 2)
        self.zh, self.x, self.t = lax.div(t, 4), lax.rem(t, 4), t
        self.m = m
        self.g = self.y * 2 + self.c
        x, c = self.x, self.c
        self.xp = (1 - c) * (x + 1 - 2 * lax.rem(x, 2)) + c * (3 - x)
        self.xq = c * (x + 1 - 2 * lax.rem(x, 2)) + (1 - c) * (3 - x)
        self.zp = 1 - self.zh
        self.tq = self.zh * 4 + self.xq

    def peer(self, dy, dc):
        yt, ct = lax.rem(self.y + dy, 4), lax.rem(self.c + dc, 2)
        yf = lax.rem(self.y + 4 - dy, 4)
        to = (self.zl * 8 + yt * 2 + ct, self.t)
        return to, yt * 2 + ct, yf * 2 + ct

    def plane(self, d):
        zt, zf = lax.rem(self.zl + d, 4), lax.rem(self.zl + 4 - d, 4)
        return (zt * 8 + self.g, self.t), zf

    def sibling(self):
        return (self.zl * 8 + self.y * 2 + 1 - self.c, self.t)

    def across(self, x_side, z_side):
        x = self.xp if x_side else self.x
        z = self.zp if z_side else self.zh
        return (self.m, z * 4 + x)

    def other_pair(self):
        return (self.m, self.tq)


class Sends:
    def __init__(self):
        self.all = []

    def start(self, src, dst, send_sem, recv_sem, device):
        copy = pltpu.make_async_remote_copy(
            src_ref=src,
            dst_ref=dst,
            send_sem=send_sem,
            recv_sem=recv_sem,
            device_id=device,
            device_id_type=MESH,
        )
        copy.start()
        self.all.append(copy)
        return copy

    def finish(self):
        for copy in self.all:
            copy.wait_send()
        self.all = []


class AllReduce:
    def __init__(self, place, sends, src, rbuf, zbuf, full, ss, rs):
        self.p, self.sends = place, sends
        self.src, self.rbuf, self.zbuf, self.full = src, rbuf, zbuf, full
        self.ss, self.rs = ss, rs

    def arrived(self, dst, i):
        pltpu.make_async_remote_copy(
            src_ref=dst,
            dst_ref=dst,
            send_sem=self.ss.at[i],
            recv_sem=self.rs.at[i],
            device_id=self.p.sibling(),
            device_id_type=MESH,
        ).wait_recv()

    def step1(self):
        for i, (dy, dc) in enumerate(PEERS):
            to, j, _ = self.p.peer(dy, dc)
            self.sends.start(self.src.at[j], self.rbuf.at[i], self.ss.at[i], self.rs.at[i], to)

    def step2(self):
        for i in range(7):
            self.arrived(self.rbuf.at[i], i)
        total = self.src[self.p.g].astype(F32)
        for i in range(7):
            total += self.rbuf[i].astype(F32)
        zl = self.p.zl
        self.zbuf[zl] = total.astype(self.zbuf.dtype)
        for d in range(1, 4):
            to, _ = self.p.plane(d)
            i = 6 + d
            self.sends.start(self.zbuf.at[zl], self.zbuf.at[zl], self.ss.at[i], self.rs.at[i], to)

    def step3(self):
        for d in range(1, 4):
            _, zf = self.p.plane(d)
            self.arrived(self.zbuf.at[zf], 6 + d)
        total = self.zbuf[0].astype(F32)
        for i in range(1, 4):
            total += self.zbuf[i].astype(F32)
        g = self.p.g
        self.full[g] = total.astype(self.full.dtype)
        for i, (dy, dc) in enumerate(PEERS):
            to, _, _ = self.p.peer(dy, dc)
            k = 10 + i
            self.sends.start(self.full.at[g], self.full.at[g], self.ss.at[k], self.rs.at[k], to)

    def step4(self):
        for i, (dy, dc) in enumerate(PEERS):
            _, _, j = self.p.peer(dy, dc)
            self.arrived(self.full.at[j], 10 + i)


def attention(ar_full, w3, tok_w, on_attended):
    flat = ar_full[...].reshape(SL, 384)
    totals = jnp.sum(flat[:, 256:384], axis=1, keepdims=True)
    denom = totals + 1e-05
    tokens = flat[:, 0:128] / denom
    d_out = flat[:, 128:256]
    scale = 1.0 / (DIM**0.5)
    qkv = precise(tokens, w3[...])
    q, k, v = qkv[:, 0:128], qkv[:, 128:256], qkv[:, 256:384]
    s = precise_nt(q, k) * scale
    st = precise_nt(k, q) * scale
    dp = precise_nt(d_out, v)
    dpt = precise_nt(v, d_out)
    e = jnp.exp(s - jnp.max(s, axis=1, keepdims=True))
    p = e / jnp.sum(e, axis=1, keepdims=True)
    et = jnp.exp(st - jnp.max(st, axis=0, keepdims=True))
    pt = et / jnp.sum(et, axis=0, keepdims=True)
    on_attended(precise(p, v).astype(BF16))
    ds = p * (dp - jnp.sum(p * dp, axis=1, keepdims=True)) * scale
    dst = pt * (dpt - jnp.sum(pt * dpt, axis=0, keepdims=True)) * scale
    dv = precise(pt, d_out)
    dq = precise(ds, k)
    dk = precise(dst, q)
    tok_w[:, 0:128] = dq
    tok_w[:, 128:256] = dk
    tok_w[:, 256:384] = dv
    grad_tokens = precise_nt(tok_w[...], w3[...])
    grad_sums = (grad_tokens / denom).astype(BF16)
    prod = grad_tokens * tokens
    col = -jnp.sum(prod, axis=1, keepdims=True) / denom
    return grad_sums, col


def main_kernel(
    cells_h, cot_h, counts, fx_h, xw_h, swt_h, qw_h, kw_h, vw_h, ow_h,
    out_h, fxg_h, xg_h, sg_h, og_h,
    cells, cot, w, wo, swt, w3, fu, pf, st, xs, xr, own, outb, fxg, xg, sg, og, mt, tokw,
    acc, accb, ag, gt, at1, at2,
    a1r, a1z, a1f, a2s, a2r, a2z, a2f, a3s, a3r, a3z, a3f,
    lsem, csem, tsem, osem, wss, wrs, gss, grs, xss, xrs,
    s1, r1, s2, r2, s3, r3,
):
    p = Place()
    sends = Sends()
    last = Sends()

    def load(src, dst, sem):
        copy = pltpu.make_async_copy(src, dst, sem)
        copy.start()
        return copy

    l_fx = load(fx_h, w.at[:, 0:128], lsem.at[0])
    l_xw = load(xw_h, w.at[:, 128:256], lsem.at[1])
    l_sw = load(swt_h.at[0], swt.at[0], lsem.at[2])
    l_ow = load(ow_h, wo.at[0], lsem.at[3])
    l_cells, l_cot = [], []
    for r in range(NCHUNK):
        rows = pl.ds(r * CHUNK, CHUNK)
        l_cells.append(load(cells_h.at[rows], cells.at[rows], csem.at[r]))
        l_cot.append(load(cot_h.at[rows], cot.at[rows], tsem.at[r]))
    l_q = load(qw_h.at[0], w3.at[:, 0:128], lsem.at[4])
    l_k = load(kw_h.at[0], w3.at[:, 128:256], lsem.at[5])
    l_v = load(vw_h.at[0], w3.at[:, 256:384], lsem.at[6])

    barrier = pltpu.get_barrier_semaphore()
    friends = [p.peer(dy, dc)[0] for dy, dc in PEERS]
    friends += [p.plane(d)[0] for d in range(1, 4)]
    friends += [p.across(0, 1), p.across(1, 0), p.across(1, 1), p.other_pair()]
    for device in friends:
        pl.semaphore_signal(barrier, inc=1, device_id=device, device_id_type=MESH)

    c, y = p.c, p.y
    x_pair, z_pair = p.across(1, 0), p.across(0, 1)

    def start(i, src, dst, device):
        sends.start(src, dst, wss.at[i], wrs.at[i], device)

    def arrived(dst, ssem, rsem):
        pltpu.make_async_remote_copy(
            src_ref=dst, dst_ref=dst, send_sem=ssem, recv_sem=rsem,
            device_id=p.sibling(), device_id_type=MESH,
        ).wait_recv()

    def landed(i, dst):
        arrived(dst, wss.at[i], wrs.at[i])

    def w_part(core, quarter, lanes):
        rows = pl.ds(pl.multiple_of(core * 512 + quarter * 128, 128), 128)
        return w.at[rows, lanes]

    def w_half(core, lanes):
        return w.at[pl.ds(pl.multiple_of(core * 512, 512), 512), lanes]

    def wo_part(slot, core, quarter):
        return wo.at[slot, pl.ds(pl.multiple_of(core * 64 + quarter * 16, 16), 16), :]

    def wo_half(slot, core):
        return wo.at[slot, pl.ds(pl.multiple_of(core * 64, 64), 64), :]

    FX0, FX1, FX2 = slice(0, 256), slice(256, 512), slice(512, 768)
    F2, X2, X3, F3 = slice(512, 640), slice(640, 768), slice(768, 896), slice(896, 1024)

    def spread_w():
        landed(0, w_part(c, y, FX2))
        for d in range(1, 4):
            start(3 + d, w_part(c, y, FX2), w_part(c, y, FX2), p.peer(d, 0)[0])

    def spread_wo():
        landed(1, wo_part(2, c, y))
        for d in range(1, 4):
            start(6 + d, wo_part(2, c, y), wo_part(2, c, y), p.peer(d, 0)[0])

    def gather_w():
        for d in range(1, 4):
            landed(3 + d, w_part(c, lax.rem(y + 4 - d, 4), FX2))
        start(10, w_half(c, FX2), w_half(c, FX2), p.sibling())
        start(12, w_half(c, X2), w_half(c, X3), x_pair)

    def gather_wo():
        for d in range(1, 4):
            landed(6 + d, wo_part(2, c, lax.rem(y + 4 - d, 4)))
        start(11, wo_half(2, c), wo_half(2, c), p.sibling())

    def pass_on():
        landed(10, w_half(1 - c, FX2))
        start(13, w_half(1 - c, X2), w_half(1 - c, X3), x_pair)
        start(14, w_half(c, F2), w_half(c, F3), x_pair)
        start(15, wo_half(2, c), wo_half(3, c), x_pair)

    def pass_on_rest():
        landed(11, wo_half(2, 1 - c))
        start(16, w_half(1 - c, F2), w_half(1 - c, F3), x_pair)
        start(17, wo_half(2, 1 - c), wo_half(3, 1 - c), x_pair)

    count = counts[0]

    def big_rows(r):
        return pl.ds(pl.multiple_of(r * BIG, BIG), BIG)

    def softmax(k, first, size, mixed):
        rows = pl.ds(first, size)
        logits = dot_nt(swt[k], mixed)
        e = jnp.exp(logits - jnp.max(logits, axis=0, keepdims=True))
        lane = lax.broadcasted_iota(jnp.int32, (1, size), 1) + first
        norm = jnp.where(lane < count, 1.0 / jnp.sum(e, axis=0, keepdims=True), 0.0)
        prob = e * norm
        pf[k, :, rows] = prob
        prob_b = prob.astype(BF16)
        st[k * 128 : k * 128 + 64, rows] = prob_b
        return prob, prob_b

    acc[...] = jnp.zeros_like(acc)

    def own_rows(first, size):
        rows = pl.ds(first, size)
        parts = range(first // CHUNK, (first + size) // CHUNK)
        for r in parts:
            l_cells[r].wait()
        xf = dot(cells[rows, :], w[:, FX0]).astype(BF16)
        fu[0, rows, 0:128] = xf[:, 0:128]
        prob, prob_b = softmax(0, first, size, xf[:, 128:256])
        for r in parts:
            l_cot[r].wait()
        fu[0, rows, 128:256] = dot_nt(cot[rows, :], wo[0]).astype(BF16)
        acc[:, 0:256] += dot(prob_b, fu[0, rows, :])
        tot = acc[:, 256:384]
        for j in range(size // 128):
            tot += prob[:, j * 128 : j * 128 + 128]
        acc[:, 256:384] = tot

    l_fx.wait()
    l_xw.wait()
    l_sw.wait()
    l_ow.wait()
    own_rows(0, CHUNK)
    pl.semaphore_wait(barrier, len(friends))
    start(0, w_part(c, y, FX0), w_part(c, y, FX2), z_pair)
    start(1, wo_part(0, c, y), wo_part(2, c, y), z_pair)
    sends.start(swt.at[0], swt.at[2], gss.at[0], grs.at[0], z_pair)
    start(2, w.at[:, FX0], w.at[:, FX1], x_pair)
    sends.start(swt.at[0], swt.at[1], gss.at[1], grs.at[1], x_pair)
    start(3, wo.at[0], wo.at[1], x_pair)
    own_rows(CHUNK, ROWS - CHUNK)
    accb[...] = acc[...].reshape(8, 8, 384)
    ar1 = AllReduce(p, sends, accb, a1r, a1z, a1f, s1, r1)
    ar2 = AllReduce(p, sends, a2s, a2r, a2z, a2f, s2, r2)
    ar3 = AllReduce(p, sends, a3s, a3r, a3z, a3f, s3, r3)
    ar1.step1()

    def products(lhs_row, rhs, dst, at):
        def body(j, _):
            cols = pl.ds(pl.multiple_of(j * 512, 512), 512)
            out = dot(st[lhs_row : lhs_row + 64, :], rhs[:, cols]).astype(BF16)
            for i in range(4):
                dst[4 * j + i, :, at : at + 128] = out[:, i * 128 : i * 128 + 128]
            return 0

        lax.fori_loop(0, 2, body, 0)

    products(0, cells, a2s, 0)
    spread_w()
    ar1.step2()
    spread_wo()
    products(0, cot, a2s, 128)
    arrived(swt.at[2], gss.at[0], grs.at[0])
    sends.start(swt.at[2], swt.at[3], gss.at[2], grs.at[2], x_pair)
    def pair_body(r, _):
        rows = big_rows(r)
        xf = dot(cells[rows, :], w[:, FX1]).astype(BF16)
        fu[1, rows, 0:128] = xf[:, 0:128]
        softmax(1, pl.multiple_of(r * BIG, BIG), BIG, xf[:, 128:256])
        fu[1, rows, 128:256] = dot_nt(cot[rows, :], wo[1]).astype(BF16)
        return 0

    ar1.step3()
    arrived(swt.at[1], gss.at[1], grs.at[1])
    landed(2, w.at[:, FX1])
    landed(3, wo.at[1])
    pair_body(0, 0)
    gather_w()
    gather_wo()
    pair_body(1, 0)
    pass_on()
    l_q.wait()
    l_k.wait()
    l_v.wait()
    ar1.step4()
    readers = ((3, p.across(1, 1)), (2, z_pair), (1, x_pair))
    GS, ATT = slice(0, 128), slice(128, 256)

    def on_attended(att):
        ag[0, :, ATT] = att
        for slot, device in readers:
            i = 8 + slot
            sends.start(ag.at[0, :, ATT], ag.at[slot, :, ATT], gss.at[i], grs.at[i], device)

    gsum, col0 = attention(a1f, w3, tokw, on_attended)
    ag[0, :, GS] = gsum
    eye = (
        lax.broadcasted_iota(jnp.int32, (SL, SL), 0)
        == lax.broadcasted_iota(jnp.int32, (SL, SL), 1)
    )
    gt[0] = jnp.broadcast_to(jnp.sum(jnp.where(eye, col0, 0.0), axis=0, keepdims=True), (8, SL))
    for slot, device in readers:
        i = 1 + 2 * slot
        sends.start(ag.at[0, :, GS], ag.at[slot, :, GS], gss.at[i], grs.at[i], device)
        sends.start(gt.at[0], gt.at[slot], gss.at[i + 1], grs.at[i + 1], device)
    ar2.step1()
    pass_on_rest()

    def vjp(k, rows, gp):
        prob = pf[k, :, rows]
        mean = jnp.sum(prob * gp, axis=0, keepdims=True)
        st[k * 128 + 64 : k * 128 + 128, rows] = (prob * (gp - mean)).astype(BF16)

    def near_vjp(k, col):
        def body(r, _):
            rows = big_rows(r)
            vjp(k, rows, dot_nt(ag[k], fu[k, rows, :]) + col)
            return 0

        lax.fori_loop(0, NBIG, body, 0)

    def column(k):
        return jnp.sum(jnp.where(eye, gt[k][0:1, :], 0.0), axis=1, keepdims=True)

    near_vjp(0, col0)
    products(64, cells, a3s, 0)
    ar3.step1()
    arrived(swt.at[3], gss.at[2], grs.at[2])
    landed(12, w_half(c, X3))
    landed(13, w_half(1 - c, X3))

    def far_body(r, _):
        mixed = dot(cells[big_rows(r), :], w[:, 640:896]).astype(BF16)
        first = pl.multiple_of(r * BIG, BIG)
        softmax(2, first, BIG, mixed[:, 0:128])
        softmax(3, first, BIG, mixed[:, 128:256])
        return 0

    lax.fori_loop(0, NBIG, far_body, 0)
    ar2.step2()

    f_at = (0, 256, 512, 896)
    x_at = (128, 384, 640, 768)
    col_rows = [pl.ds(pl.multiple_of(t * 128, 128), 128) for t in (p.tq, p.t)]

    def fixed_columns(k):
        for i, rows in enumerate(col_rows):
            mt[i, :, k * 128 + 64 : k * 128 + 128] = dot_nt(
                w[rows, x_at[k] : x_at[k] + 128], swt[k]
            ).astype(BF16)

    def sum_columns(k):
        for i, rows in enumerate(col_rows):
            mt[i, :, k * 128 : k * 128 + 64] = dot_nt(
                w[rows, f_at[k] : f_at[k] + 128], ag[k, :, 0:128]
            ).astype(BF16)

    def attended_from(k):
        arrived(ag.at[k, :, ATT], gss.at[8 + k], grs.at[8 + k])

    def gradients_from(k):
        i = 1 + 2 * k
        arrived(ag.at[k, :, GS], gss.at[i], grs.at[i])
        arrived(gt.at[k], gss.at[i + 1], grs.at[i + 1])

    def centred(k, lanes):
        full = ag[k, :, lanes].astype(F32)
        return (full - jnp.mean(full, axis=0, keepdims=True)).astype(BF16)

    def fold_rows(k):
        return slice((k - 2) * 64, (k - 1) * 64)

    for k in range(4):
        fixed_columns(k)
    sum_columns(0)
    ar3.step2()
    attended_from(1)
    gradients_from(1)
    near_vjp(1, column(1))
    sum_columns(1)
    landed(14, w_half(c, F3))
    landed(15, wo_half(3, c))
    landed(16, w_half(1 - c, F3))
    landed(17, wo_half(3, 1 - c))
    attended_from(2)
    attended_from(3)
    for k in (2, 3):
        at2[fold_rows(k), :] = dot(centred(k, ATT), wo[k]).astype(BF16)
    gradients_from(2)
    gradients_from(3)
    for k in (2, 3):
        lanes = slice(f_at[k], f_at[k] + 128)
        at1[fold_rows(k), :] = dot_nt(centred(k, GS), w[:, lanes]).astype(BF16)
    for k in (2, 3):
        sum_columns(k)
    gcol = [column(k) for k in (2, 3)]
    for r in range(NLATE):
        rows = pl.ds(EDGES[r], EDGES[r + 1] - EDGES[r])
        gp = dot_nt(at1[...], cells[rows, :]) + dot_nt(at2[...], cot[rows, :])
        for k in (2, 3):
            vjp(k, rows, gp[(k - 2) * 64 : (k - 1) * 64, :] + gcol[k - 2])
        xs[:, rows] = dot(mt[0], st[:, rows]).astype(BF16)
        part = slice(EDGES[r], EDGES[r + 1])
        last.start(xs.at[:, part], xr.at[:, part], xss.at[r], xrs.at[r], p.other_pair())
        if r == 1:
            ar2.step3()
    ar3.step3()
    for r in range(NCHUNK):
        rows = pl.ds(r * CHUNK, CHUNK)
        own[:, rows] = dot(mt[1], st[:, rows])
    tn = (((0,), (0,)), ((), ()))
    outs = []
    ar2.step4()
    gs = ag[0, :, 0:128]
    att_t = ag[0, :, 128:256].astype(F32).T.astype(BF16)
    for j in range(8):
        cols = slice(j * 128, j * 128 + 128)
        fxg[cols, :] = lax.dot_general(a2f[j, :, 0:128], gs, tn, preferred_element_type=F32)
        og[:, cols] = dot(att_t, a2f[j, :, 128:256])
    outs.append(load(fxg, fxg_h, osem.at[0]))
    outs.append(load(og, og_h, osem.at[1]))
    for r in range(NLATE):
        rows = pl.ds(EDGES[r], EDGES[r + 1] - EDGES[r])
        arrived(xr.at[:, slice(EDGES[r], EDGES[r + 1])], xss.at[r], xrs.at[r])
        total = own[:, rows] + xr[:, rows].astype(F32)
        outb[rows, :] = total.T.astype(BF16)
        outs.append(load(outb.at[rows], out_h.at[rows], osem.at[4 + r]))
        if r == 2:
            ar3.step4()
            swt0 = swt[0]
            total = jnp.zeros((SL, DIM), F32)
            for j in range(8):
                cols = slice(j * 128, j * 128 + 128)
                xg[cols, :] = lax.dot_general(a3f[j], swt0, tn, preferred_element_type=F32)
                total += dot(a3f[j], w[cols, 128:256])
            sg[0] = total
            outs.append(load(xg, xg_h, osem.at[2]))
            outs.append(load(sg, sg_h, osem.at[3]))
            sends.finish()
    for copy in outs:
        copy.wait()
    last.finish()


def finish_kernel(*refs):
    src, dst, held, sem = refs[0:5], refs[5:10], refs[10:15], refs[15]
    inward = [pltpu.make_async_copy(src[i], held[i], sem.at[i]) for i in range(5)]
    outward = [pltpu.make_async_copy(held[i], dst[i], sem.at[5 + i]) for i in range(5)]
    for copy in inward:
        copy.start()
    for i in range(5):
        inward[i].wait()
        outward[i].start()
    for copy in outward:
        copy.wait()


def shards(cells, cot, counts, fx_w, x_w, s_w, q_w, k_w, v_w, o_w):
    hbm = pl.BlockSpec(memory_space=pl.ANY)
    sds = jax.ShapeDtypeStruct
    dma = pltpu.SemaphoreType.DMA
    V = pltpu.VMEM
    swt = jnp.swapaxes(s_w, 1, 2)
    limit = 60 * 1024 * 1024
    shapes = (
        sds((ROWS, DIM), BF16),
        sds((WIDTH, DIM), F32),
        sds((WIDTH, DIM), F32),
        sds((1, SL, DIM), F32),
        sds((DIM, WIDTH), F32),
    )
    held = [V(a.shape, a.dtype) for a in shapes]
    outs = pl.pallas_call(
        main_kernel,
        name="layer",
        out_shape=shapes,
        in_specs=[hbm, hbm, pl.BlockSpec(memory_space=pltpu.SMEM)] + [hbm] * 7,
        out_specs=[hbm] * 5,
        scratch_shapes=[
            V((ROWS, WIDTH), BF16),
            V((ROWS, WIDTH), BF16),
            V((WIDTH, 1024), BF16),
            V((4, DIM, WIDTH), BF16),
            V((4, SL, 128), BF16),
            V((DIM, 384), F32),
            V((2, ROWS, 256), BF16),
            V((4, SL, ROWS), F32),
            V((512, ROWS), BF16),
            V((DIM, ROWS), BF16),
            V((DIM, ROWS), BF16),
            V((DIM, ROWS), F32),
            *held,
            V((2, DIM, 512), BF16),
            V((SL, 384), F32),
            V((SL, 384), F32),
            V((8, 8, 384), F32),
            V((4, SL, 256), BF16),
            V((4, 8, SL), F32),
            V((128, WIDTH), BF16),
            V((128, WIDTH), BF16),
            V((7, 8, 384), F32),
            V((4, 8, 384), F32),
            V((8, 8, 384), F32),
            V((8, SL, 256), BF16),
            V((7, SL, 256), BF16),
            V((4, SL, 256), BF16),
            V((8, SL, 256), BF16),
            V((8, SL, 128), BF16),
            V((7, SL, 128), BF16),
            V((4, SL, 128), BF16),
            V((8, SL, 128), BF16),
            dma((7,)),
            dma((NCHUNK,)),
            dma((NCHUNK,)),
            dma((4 + NLATE,)),
            dma((18,)),
            dma((18,)),
            dma((12,)),
            dma((12,)),
            dma((NLATE,)),
            dma((NLATE,)),
        ]
        + [dma((17,))] * 6,
        compiler_params=pltpu.CompilerParams(
            collective_id=0, has_side_effects=True, vmem_limit_bytes=limit
        ),
    )(cells, cot, counts, fx_w, x_w, swt, q_w, k_w, v_w, o_w)
    outs = pl.pallas_call(
        finish_kernel,
        name="grads",
        out_shape=shapes,
        in_specs=[hbm] * 5,
        out_specs=[hbm] * 5,
        scratch_shapes=[*held, dma((10,))],
        compiler_params=pltpu.CompilerParams(vmem_limit_bytes=limit),
    )(*outs)
    return outs[0], outs[1], outs[2], jnp.swapaxes(outs[3], 1, 2), outs[4]


def solution(mesh):
    in_specs = (
        P("mesh", None),
        P("mesh", None),
        P("mesh"),
        P(None, "tensor"),
        P(None, "tensor"),
        P("tensor", None, None),
        P("tensor", None, None),
        P("tensor", None, None),
        P("tensor", None, None),
        P("tensor", None),
    )
    out_specs = (
        P("mesh", "tensor"),
        P(None, "tensor"),
        P(None, "tensor"),
        P("tensor", None, None),
        P("tensor", None),
    )
    return jax.shard_map(shards, mesh=mesh, in_specs=in_specs, out_specs=out_specs, check_vma=False)
```

```python
import jax
import jax.numpy as jnp
from jax import lax
from jax.experimental import pallas as pl
from jax.experimental.pallas import tpu as pltpu
from jax.sharding import PartitionSpec as P

MESH = pl.DeviceIdType.MESH
F32 = jnp.float32
BF16 = jnp.bfloat16
ROWS = 2048
WIDTH = 1024
DIM = 128
SL = 64
CHUNK = 512
NCHUNK = ROWS // CHUNK
EDGES = (0, 512, 1024, 1536, 2048)
NLATE = len(EDGES) - 1
BIG = 1024
NBIG = ROWS // BIG
PEERS = [(2, 1), (2, 0), (1, 1), (3, 1), (1, 0), (3, 0), (0, 1)]
NT = (((1,), (1,)), ((), ()))


def dot(a, b):
    return jnp.dot(a, b, preferred_element_type=F32)


def dot_nt(a, b):
    return lax.dot_general(a, b, NT, preferred_element_type=F32)


def precise(a, b):
    return jnp.dot(a, b, preferred_element_type=F32, precision=lax.Precision.HIGHEST)


def precise_nt(a, b):
    return lax.dot_general(
        a, b, NT, preferred_element_type=F32, precision=lax.Precision.HIGHEST
    )


class Place:
    def __init__(self):
        m = lax.axis_index("mesh")
        t = lax.axis_index("tensor")
        self.zl, self.y, self.c = lax.div(m, 8), lax.rem(lax.div(m, 2), 4), lax.rem(m, 2)
        self.zh, self.x, self.t = lax.div(t, 4), lax.rem(t, 4), t
        self.m = m
        self.g = self.y * 2 + self.c
        x, c = self.x, self.c
        self.xp = (1 - c) * (x + 1 - 2 * lax.rem(x, 2)) + c * (3 - x)
        self.xq = c * (x + 1 - 2 * lax.rem(x, 2)) + (1 - c) * (3 - x)
        self.zp = 1 - self.zh
        self.tq = self.zh * 4 + self.xq

    def peer(self, dy, dc):
        yt, ct = lax.rem(self.y + dy, 4), lax.rem(self.c + dc, 2)
        yf = lax.rem(self.y + 4 - dy, 4)
        to = (self.zl * 8 + yt * 2 + ct, self.t)
        return to, yt * 2 + ct, yf * 2 + ct

    def plane(self, d):
        zt, zf = lax.rem(self.zl + d, 4), lax.rem(self.zl + 4 - d, 4)
        return (zt * 8 + self.g, self.t), zf

    def sibling(self):
        return (self.zl * 8 + self.y * 2 + 1 - self.c, self.t)

    def across(self, x_side, z_side):
        x = self.xp if x_side else self.x
        z = self.zp if z_side else self.zh
        return (self.m, z * 4 + x)

    def other_pair(self):
        return (self.m, self.tq)


class Sends:
    def __init__(self):
        self.all = []

    def start(self, src, dst, send_sem, recv_sem, device):
        copy = pltpu.make_async_remote_copy(
            src_ref=src,
            dst_ref=dst,
            send_sem=send_sem,
            recv_sem=recv_sem,
            device_id=device,
            device_id_type=MESH,
        )
        copy.start()
        self.all.append(copy)
        return copy

    def finish(self):
        for copy in self.all:
            copy.wait_send()
        self.all = []


class AllReduce:
    def __init__(self, place, sends, src, rbuf, zbuf, full, ss, rs):
        self.p, self.sends = place, sends
        self.src, self.rbuf, self.zbuf, self.full = src, rbuf, zbuf, full
        self.ss, self.rs = ss, rs

    def arrived(self, dst, i):
        pltpu.make_async_remote_copy(
            src_ref=dst,
            dst_ref=dst,
            send_sem=self.ss.at[i],
            recv_sem=self.rs.at[i],
            device_id=self.p.sibling(),
            device_id_type=MESH,
        ).wait_recv()

    def step1(self):
        for i, (dy, dc) in enumerate(PEERS):
            to, j, _ = self.p.peer(dy, dc)
            self.sends.start(self.src.at[j], self.rbuf.at[i], self.ss.at[i], self.rs.at[i], to)

    def step2(self):
        for i in range(7):
            self.arrived(self.rbuf.at[i], i)
        total = self.src[self.p.g].astype(F32)
        for i in range(7):
            total += self.rbuf[i].astype(F32)
        zl = self.p.zl
        self.zbuf[zl] = total.astype(self.zbuf.dtype)
        for d in range(1, 4):
            to, _ = self.p.plane(d)
            i = 6 + d
            self.sends.start(self.zbuf.at[zl], self.zbuf.at[zl], self.ss.at[i], self.rs.at[i], to)

    def step3(self):
        for d in range(1, 4):
            _, zf = self.p.plane(d)
            self.arrived(self.zbuf.at[zf], 6 + d)
        total = self.zbuf[0].astype(F32)
        for i in range(1, 4):
            total += self.zbuf[i].astype(F32)
        g = self.p.g
        self.full[g] = total.astype(self.full.dtype)
        for i, (dy, dc) in enumerate(PEERS):
            to, _, _ = self.p.peer(dy, dc)
            k = 10 + i
            self.sends.start(self.full.at[g], self.full.at[g], self.ss.at[k], self.rs.at[k], to)

    def step4(self):
        for i, (dy, dc) in enumerate(PEERS):
            _, _, j = self.p.peer(dy, dc)
            self.arrived(self.full.at[j], 10 + i)


def attention(ar_full, w3, tok_w, on_attended):
    flat = ar_full[...].reshape(SL, 384)
    totals = jnp.sum(flat[:, 256:384], axis=1, keepdims=True)
    denom = totals + 1e-05
    tokens = flat[:, 0:128] / denom
    d_out = flat[:, 128:256]
    scale = 1.0 / (DIM**0.5)
    qkv = precise(tokens, w3[...])
    q, k, v = qkv[:, 0:128], qkv[:, 128:256], qkv[:, 256:384]
    s = precise_nt(q, k) * scale
    st = precise_nt(k, q) * scale
    dp = precise_nt(d_out, v)
    dpt = precise_nt(v, d_out)
    e = jnp.exp(s - jnp.max(s, axis=1, keepdims=True))
    p = e / jnp.sum(e, axis=1, keepdims=True)
    et = jnp.exp(st - jnp.max(st, axis=0, keepdims=True))
    pt = et / jnp.sum(et, axis=0, keepdims=True)
    on_attended(precise(p, v).astype(BF16))
    ds = p * (dp - jnp.sum(p * dp, axis=1, keepdims=True)) * scale
    dst = pt * (dpt - jnp.sum(pt * dpt, axis=0, keepdims=True)) * scale
    dv = precise(pt, d_out)
    dq = precise(ds, k)
    dk = precise(dst, q)
    tok_w[:, 0:128] = dq
    tok_w[:, 128:256] = dk
    tok_w[:, 256:384] = dv
    grad_tokens = precise_nt(tok_w[...], w3[...])
    grad_sums = (grad_tokens / denom).astype(BF16)
    prod = grad_tokens * tokens
    col = -jnp.sum(prod, axis=1, keepdims=True) / denom
    return grad_sums, col


def main_kernel(
    cells_h, cot_h, counts, fx_h, xw_h, swt_h, qw_h, kw_h, vw_h, ow_h,
    out_h, fxg_h, xg_h, sg_h, og_h,
    cells, cot, w, wo, swt, w3, fu, pf, st, xs, xr, own, outb, fxg, xg, sg, og, mt, tokw,
    acc, accb, ag, gt, at1, at2,
    a1r, a1z, a1f, a2s, a2r, a2z, a2f, a3s, a3r, a3z, a3f,
    lsem, csem, tsem, osem, wss, wrs, gss, grs, xss, xrs,
    s1, r1, s2, r2, s3, r3,
):
    p = Place()
    sends = Sends()
    last = Sends()

    def load(src, dst, sem):
        copy = pltpu.make_async_copy(src, dst, sem)
        copy.start()
        return copy

    l_fx = load(fx_h, w.at[:, 0:128], lsem.at[0])
    l_xw = load(xw_h, w.at[:, 128:256], lsem.at[1])
    l_sw = load(swt_h.at[0], swt.at[0], lsem.at[2])
    l_ow = load(ow_h, wo.at[0], lsem.at[3])
    l_cells, l_cot = [], []
    for r in range(NCHUNK):
        rows = pl.ds(r * CHUNK, CHUNK)
        l_cells.append(load(cells_h.at[rows], cells.at[rows], csem.at[r]))
        l_cot.append(load(cot_h.at[rows], cot.at[rows], tsem.at[r]))
    l_q = load(qw_h.at[0], w3.at[:, 0:128], lsem.at[4])
    l_k = load(kw_h.at[0], w3.at[:, 128:256], lsem.at[5])
    l_v = load(vw_h.at[0], w3.at[:, 256:384], lsem.at[6])

    barrier = pltpu.get_barrier_semaphore()
    friends = [p.peer(dy, dc)[0] for dy, dc in PEERS]
    friends += [p.plane(d)[0] for d in range(1, 4)]
    friends += [p.across(0, 1), p.across(1, 0), p.across(1, 1), p.other_pair()]
    for device in friends:
        pl.semaphore_signal(barrier, inc=1, device_id=device, device_id_type=MESH)

    c, y = p.c, p.y
    x_pair, z_pair = p.across(1, 0), p.across(0, 1)

    def start(i, src, dst, device):
        sends.start(src, dst, wss.at[i], wrs.at[i], device)

    def arrived(dst, ssem, rsem):
        pltpu.make_async_remote_copy(
            src_ref=dst, dst_ref=dst, send_sem=ssem, recv_sem=rsem,
            device_id=p.sibling(), device_id_type=MESH,
        ).wait_recv()

    def landed(i, dst):
        arrived(dst, wss.at[i], wrs.at[i])

    def w_part(core, quarter, lanes):
        rows = pl.ds(pl.multiple_of(core * 512 + quarter * 128, 128), 128)
        return w.at[rows, lanes]

    def w_half(core, lanes):
        return w.at[pl.ds(pl.multiple_of(core * 512, 512), 512), lanes]

    def wo_part(slot, core, quarter):
        return wo.at[slot, pl.ds(pl.multiple_of(core * 64 + quarter * 16, 16), 16), :]

    def wo_half(slot, core):
        return wo.at[slot, pl.ds(pl.multiple_of(core * 64, 64), 64), :]

    FX0, FX1, FX2 = slice(0, 256), slice(256, 512), slice(512, 768)
    F2, X2, X3, F3 = slice(512, 640), slice(640, 768), slice(768, 896), slice(896, 1024)

    def spread_w():
        landed(0, w_part(c, y, FX2))
        for d in range(1, 4):
            start(3 + d, w_part(c, y, FX2), w_part(c, y, FX2), p.peer(d, 0)[0])
        start(12, w_part(c, y, X2), w_part(c, y, X3), x_pair)
        start(14, w_part(c, y, F2), w_part(c, y, F3), x_pair)

    def spread_wo():
        landed(1, wo_part(2, c, y))
        for d in range(1, 4):
            start(6 + d, wo_part(2, c, y), wo_part(2, c, y), p.peer(d, 0)[0])
        start(15, wo_part(2, c, y), wo_part(3, c, y), x_pair)

    quarters = [(d, lax.rem(y + 4 - d, 4)) for d in range(1, 4)]

    def gather_w():
        for d in range(1, 4):
            landed(3 + d, w_part(c, lax.rem(y + 4 - d, 4), FX2))
        start(10, w_half(c, FX2), w_half(c, FX2), p.sibling())
        for d, q in quarters:
            start(17 + d, w_part(c, q, X2), w_part(c, q, X3), x_pair)

    def gather_wo():
        for d in range(1, 4):
            landed(6 + d, wo_part(2, c, lax.rem(y + 4 - d, 4)))
        start(11, wo_half(2, c), wo_half(2, c), p.sibling())

    def pass_on():
        landed(10, w_half(1 - c, FX2))
        start(13, w_half(1 - c, X2), w_half(1 - c, X3), x_pair)
        for d, q in quarters:
            start(20 + d, w_part(c, q, F2), w_part(c, q, F3), x_pair)
            start(23 + d, wo_part(2, c, q), wo_part(3, c, q), x_pair)

    def pass_on_rest():
        landed(11, wo_half(2, 1 - c))
        start(16, w_half(1 - c, F2), w_half(1 - c, F3), x_pair)
        start(17, wo_half(2, 1 - c), wo_half(3, 1 - c), x_pair)

    count = counts[0]

    def big_rows(r):
        return pl.ds(pl.multiple_of(r * BIG, BIG), BIG)

    def softmax(k, first, size, mixed):
        rows = pl.ds(first, size)
        logits = dot_nt(swt[k], mixed)
        e = jnp.exp(logits - jnp.max(logits, axis=0, keepdims=True))
        lane = lax.broadcasted_iota(jnp.int32, (1, size), 1) + first
        norm = jnp.where(lane < count, 1.0 / jnp.sum(e, axis=0, keepdims=True), 0.0)
        prob = e * norm
        pf[k, :, rows] = prob
        prob_b = prob.astype(BF16)
        st[k * 128 : k * 128 + 64, rows] = prob_b
        return prob, prob_b

    acc[...] = jnp.zeros_like(acc)

    def own_rows(first, size):
        rows = pl.ds(first, size)
        parts = range(first // CHUNK, (first + size) // CHUNK)
        for r in parts:
            l_cells[r].wait()
        xf = dot(cells[rows, :], w[:, FX0]).astype(BF16)
        fu[0, rows, 0:128] = xf[:, 0:128]
        prob, prob_b = softmax(0, first, size, xf[:, 128:256])
        for r in parts:
            l_cot[r].wait()
        fu[0, rows, 128:256] = dot_nt(cot[rows, :], wo[0]).astype(BF16)
        acc[:, 0:256] += dot(prob_b, fu[0, rows, :])
        tot = acc[:, 256:384]
        for j in range(size // 128):
            tot += prob[:, j * 128 : j * 128 + 128]
        acc[:, 256:384] = tot

    l_fx.wait()
    l_xw.wait()
    l_sw.wait()
    l_ow.wait()
    own_rows(0, CHUNK)
    pl.semaphore_wait(barrier, len(friends))
    start(0, w_part(c, y, FX0), w_part(c, y, FX2), z_pair)
    start(1, wo_part(0, c, y), wo_part(2, c, y), z_pair)
    sends.start(swt.at[0], swt.at[2], gss.at[0], grs.at[0], z_pair)
    start(2, w.at[:, FX0], w.at[:, FX1], x_pair)
    sends.start(swt.at[0], swt.at[1], gss.at[1], grs.at[1], x_pair)
    start(3, wo.at[0], wo.at[1], x_pair)
    own_rows(CHUNK, ROWS - CHUNK)
    accb[...] = acc[...].reshape(8, 8, 384)
    ar1 = AllReduce(p, sends, accb, a1r, a1z, a1f, s1, r1)
    ar2 = AllReduce(p, sends, a2s, a2r, a2z, a2f, s2, r2)
    ar3 = AllReduce(p, sends, a3s, a3r, a3z, a3f, s3, r3)
    ar1.step1()

    def products(lhs_row, rhs, dst, at):
        def body(j, _):
            cols = pl.ds(pl.multiple_of(j * 512, 512), 512)
            out = dot(st[lhs_row : lhs_row + 64, :], rhs[:, cols]).astype(BF16)
            for i in range(4):
                dst[4 * j + i, :, at : at + 128] = out[:, i * 128 : i * 128 + 128]
            return 0

        lax.fori_loop(0, 2, body, 0)

    products(0, cells, a2s, 0)
    spread_w()
    ar1.step2()
    spread_wo()
    products(0, cot, a2s, 128)
    arrived(swt.at[2], gss.at[0], grs.at[0])
    sends.start(swt.at[2], swt.at[3], gss.at[2], grs.at[2], x_pair)
    def pair_body(r, _):
        rows = big_rows(r)
        xf = dot(cells[rows, :], w[:, FX1]).astype(BF16)
        fu[1, rows, 0:128] = xf[:, 0:128]
        softmax(1, pl.multiple_of(r * BIG, BIG), BIG, xf[:, 128:256])
        fu[1, rows, 128:256] = dot_nt(cot[rows, :], wo[1]).astype(BF16)
        return 0

    ar1.step3()
    arrived(swt.at[1], gss.at[1], grs.at[1])
    landed(2, w.at[:, FX1])
    landed(3, wo.at[1])
    pair_body(0, 0)
    gather_w()
    gather_wo()
    pair_body(1, 0)
    pass_on()
    l_q.wait()
    l_k.wait()
    l_v.wait()
    ar1.step4()
    readers = ((3, p.across(1, 1)), (2, z_pair), (1, x_pair))
    GS, ATT = slice(0, 128), slice(128, 256)

    def on_attended(att):
        ag[0, :, ATT] = att
        for slot, device in readers:
            i = 8 + slot
            sends.start(ag.at[0, :, ATT], ag.at[slot, :, ATT], gss.at[i], grs.at[i], device)

    gsum, col0 = attention(a1f, w3, tokw, on_attended)
    ag[0, :, GS] = gsum
    eye = (
        lax.broadcasted_iota(jnp.int32, (SL, SL), 0)
        == lax.broadcasted_iota(jnp.int32, (SL, SL), 1)
    )
    gt[0] = jnp.broadcast_to(jnp.sum(jnp.where(eye, col0, 0.0), axis=0, keepdims=True), (8, SL))
    for slot, device in readers:
        i = 1 + 2 * slot
        sends.start(ag.at[0, :, GS], ag.at[slot, :, GS], gss.at[i], grs.at[i], device)
        sends.start(gt.at[0], gt.at[slot], gss.at[i + 1], grs.at[i + 1], device)
    ar2.step1()
    pass_on_rest()

    def vjp(k, rows, gp):
        prob = pf[k, :, rows]
        mean = jnp.sum(prob * gp, axis=0, keepdims=True)
        st[k * 128 + 64 : k * 128 + 128, rows] = (prob * (gp - mean)).astype(BF16)

    def near_vjp(k, col):
        def body(r, _):
            rows = big_rows(r)
            vjp(k, rows, dot_nt(ag[k], fu[k, rows, :]) + col)
            return 0

        lax.fori_loop(0, NBIG, body, 0)

    def column(k):
        return jnp.sum(jnp.where(eye, gt[k][0:1, :], 0.0), axis=1, keepdims=True)

    near_vjp(0, col0)
    products(64, cells, a3s, 0)
    ar3.step1()
    arrived(swt.at[3], gss.at[2], grs.at[2])
    landed(12, w_part(c, y, X3))
    for d, q in quarters:
        landed(17 + d, w_part(c, q, X3))
    landed(13, w_half(1 - c, X3))

    def far_body(r, _):
        mixed = dot(cells[big_rows(r), :], w[:, 640:896]).astype(BF16)
        first = pl.multiple_of(r * BIG, BIG)
        softmax(2, first, BIG, mixed[:, 0:128])
        softmax(3, first, BIG, mixed[:, 128:256])
        return 0

    lax.fori_loop(0, NBIG, far_body, 0)
    ar2.step2()

    f_at = (0, 256, 512, 896)
    x_at = (128, 384, 640, 768)
    col_rows = [pl.ds(pl.multiple_of(t * 128, 128), 128) for t in (p.tq, p.t)]

    def fixed_columns(k):
        for i, rows in enumerate(col_rows):
            mt[i, :, k * 128 + 64 : k * 128 + 128] = dot_nt(
                w[rows, x_at[k] : x_at[k] + 128], swt[k]
            ).astype(BF16)

    def sum_columns(k):
        for i, rows in enumerate(col_rows):
            mt[i, :, k * 128 : k * 128 + 64] = dot_nt(
                w[rows, f_at[k] : f_at[k] + 128], ag[k, :, 0:128]
            ).astype(BF16)

    def attended_from(k):
        arrived(ag.at[k, :, ATT], gss.at[8 + k], grs.at[8 + k])

    def gradients_from(k):
        i = 1 + 2 * k
        arrived(ag.at[k, :, GS], gss.at[i], grs.at[i])
        arrived(gt.at[k], gss.at[i + 1], grs.at[i + 1])

    def centred(k, lanes):
        full = ag[k, :, lanes].astype(F32)
        return (full - jnp.mean(full, axis=0, keepdims=True)).astype(BF16)

    def fold_rows(k):
        return slice((k - 2) * 64, (k - 1) * 64)

    for k in range(4):
        fixed_columns(k)
    sum_columns(0)
    ar3.step2()
    attended_from(1)
    gradients_from(1)
    near_vjp(1, column(1))
    sum_columns(1)
    landed(14, w_part(c, y, F3))
    landed(15, wo_part(3, c, y))
    for d, q in quarters:
        landed(20 + d, w_part(c, q, F3))
        landed(23 + d, wo_part(3, c, q))
    landed(16, w_half(1 - c, F3))
    landed(17, wo_half(3, 1 - c))
    attended_from(2)
    attended_from(3)
    for k in (2, 3):
        at2[fold_rows(k), :] = dot(centred(k, ATT), wo[k]).astype(BF16)
    gradients_from(2)
    gradients_from(3)
    for k in (2, 3):
        lanes = slice(f_at[k], f_at[k] + 128)
        at1[fold_rows(k), :] = dot_nt(centred(k, GS), w[:, lanes]).astype(BF16)
    for k in (2, 3):
        sum_columns(k)
    gcol = [column(k) for k in (2, 3)]
    for r in range(NLATE):
        rows = pl.ds(EDGES[r], EDGES[r + 1] - EDGES[r])
        gp = dot_nt(at1[...], cells[rows, :]) + dot_nt(at2[...], cot[rows, :])
        for k in (2, 3):
            vjp(k, rows, gp[(k - 2) * 64 : (k - 1) * 64, :] + gcol[k - 2])
        xs[:, rows] = dot(mt[0], st[:, rows]).astype(BF16)
        part = slice(EDGES[r], EDGES[r + 1])
        last.start(xs.at[:, part], xr.at[:, part], xss.at[r], xrs.at[r], p.other_pair())
        if r == 1:
            ar2.step3()
    ar3.step3()
    for r in range(NCHUNK):
        rows = pl.ds(r * CHUNK, CHUNK)
        own[:, rows] = dot(mt[1], st[:, rows])
    tn = (((0,), (0,)), ((), ()))
    outs = []
    ar2.step4()
    gs = ag[0, :, 0:128]
    att_t = ag[0, :, 128:256].astype(F32).T.astype(BF16)
    for j in range(8):
        cols = slice(j * 128, j * 128 + 128)
        fxg[cols, :] = lax.dot_general(a2f[j, :, 0:128], gs, tn, preferred_element_type=F32)
        og[:, cols] = dot(att_t, a2f[j, :, 128:256])
    outs.append(load(fxg, fxg_h, osem.at[0]))
    outs.append(load(og, og_h, osem.at[1]))
    for r in range(NLATE):
        rows = pl.ds(EDGES[r], EDGES[r + 1] - EDGES[r])
        arrived(xr.at[:, slice(EDGES[r], EDGES[r + 1])], xss.at[r], xrs.at[r])
        total = own[:, rows] + xr[:, rows].astype(F32)
        outb[rows, :] = total.T.astype(BF16)
        outs.append(load(outb.at[rows], out_h.at[rows], osem.at[4 + r]))
        if r == 2:
            ar3.step4()
            swt0 = swt[0]
            total = jnp.zeros((SL, DIM), F32)
            for j in range(8):
                cols = slice(j * 128, j * 128 + 128)
                xg[cols, :] = lax.dot_general(a3f[j], swt0, tn, preferred_element_type=F32)
                total += dot(a3f[j], w[cols, 128:256])
            sg[0] = total
            outs.append(load(xg, xg_h, osem.at[2]))
            outs.append(load(sg, sg_h, osem.at[3]))
            sends.finish()
    for copy in outs:
        copy.wait()
    last.finish()


def finish_kernel(*refs):
    src, dst, held, sem = refs[0:5], refs[5:10], refs[10:15], refs[15]
    inward = [pltpu.make_async_copy(src[i], held[i], sem.at[i]) for i in range(5)]
    outward = [pltpu.make_async_copy(held[i], dst[i], sem.at[5 + i]) for i in range(5)]
    for copy in inward:
        copy.start()
    for i in range(5):
        inward[i].wait()
        outward[i].start()
    for copy in outward:
        copy.wait()


def shards(cells, cot, counts, fx_w, x_w, s_w, q_w, k_w, v_w, o_w):
    hbm = pl.BlockSpec(memory_space=pl.ANY)
    sds = jax.ShapeDtypeStruct
    dma = pltpu.SemaphoreType.DMA
    V = pltpu.VMEM
    swt = jnp.swapaxes(s_w, 1, 2)
    limit = 60 * 1024 * 1024
    shapes = (
        sds((ROWS, DIM), BF16),
        sds((WIDTH, DIM), F32),
        sds((WIDTH, DIM), F32),
        sds((1, SL, DIM), F32),
        sds((DIM, WIDTH), F32),
    )
    held = [V(a.shape, a.dtype) for a in shapes]
    outs = pl.pallas_call(
        main_kernel,
        name="layer",
        out_shape=shapes,
        in_specs=[hbm, hbm, pl.BlockSpec(memory_space=pltpu.SMEM)] + [hbm] * 7,
        out_specs=[hbm] * 5,
        scratch_shapes=[
            V((ROWS, WIDTH), BF16),
            V((ROWS, WIDTH), BF16),
            V((WIDTH, 1024), BF16),
            V((4, DIM, WIDTH), BF16),
            V((4, SL, 128), BF16),
            V((DIM, 384), F32),
            V((2, ROWS, 256), BF16),
            V((4, SL, ROWS), F32),
            V((512, ROWS), BF16),
            V((DIM, ROWS), BF16),
            V((DIM, ROWS), BF16),
            V((DIM, ROWS), F32),
            *held,
            V((2, DIM, 512), BF16),
            V((SL, 384), F32),
            V((SL, 384), F32),
            V((8, 8, 384), F32),
            V((4, SL, 256), BF16),
            V((4, 8, SL), F32),
            V((128, WIDTH), BF16),
            V((128, WIDTH), BF16),
            V((7, 8, 384), F32),
            V((4, 8, 384), F32),
            V((8, 8, 384), F32),
            V((8, SL, 256), BF16),
            V((7, SL, 256), BF16),
            V((4, SL, 256), BF16),
            V((8, SL, 256), BF16),
            V((8, SL, 128), BF16),
            V((7, SL, 128), BF16),
            V((4, SL, 128), BF16),
            V((8, SL, 128), BF16),
            dma((7,)),
            dma((NCHUNK,)),
            dma((NCHUNK,)),
            dma((4 + NLATE,)),
            dma((27,)),
            dma((27,)),
            dma((12,)),
            dma((12,)),
            dma((NLATE,)),
            dma((NLATE,)),
        ]
        + [dma((17,))] * 6,
        compiler_params=pltpu.CompilerParams(
            collective_id=0, has_side_effects=True, vmem_limit_bytes=limit
        ),
    )(cells, cot, counts, fx_w, x_w, swt, q_w, k_w, v_w, o_w)
    outs = pl.pallas_call(
        finish_kernel,
        name="grads",
        out_shape=shapes,
        in_specs=[hbm] * 5,
        out_specs=[hbm] * 5,
        scratch_shapes=[*held, dma((10,))],
        compiler_params=pltpu.CompilerParams(vmem_limit_bytes=limit),
    )(*outs)
    return outs[0], outs[1], outs[2], jnp.swapaxes(outs[3], 1, 2), outs[4]


def solution(mesh):
    in_specs = (
        P("mesh", None),
        P("mesh", None),
        P("mesh"),
        P(None, "tensor"),
        P(None, "tensor"),
        P("tensor", None, None),
        P("tensor", None, None),
        P("tensor", None, None),
        P("tensor", None, None),
        P("tensor", None),
    )
    out_specs = (
        P("mesh", "tensor"),
        P(None, "tensor"),
        P(None, "tensor"),
        P("tensor", None, None),
        P("tensor", None),
    )
    return jax.shard_map(shards, mesh=mesh, in_specs=in_specs, out_specs=out_specs, check_vma=False)
```

```python
import jax
import jax.numpy as jnp
from jax import lax
from jax.experimental import pallas as pl
from jax.experimental.pallas import tpu as pltpu
from jax.sharding import PartitionSpec as P

MESH = pl.DeviceIdType.MESH
F32 = jnp.float32
BF16 = jnp.bfloat16
ROWS = 2048
WIDTH = 1024
DIM = 128
SL = 64
CHUNK = 512
NCHUNK = ROWS // CHUNK
EDGES = (0, 512, 1024, 1536, 2048)
NLATE = len(EDGES) - 1
BIG = 1024
NBIG = ROWS // BIG
PEERS = [(2, 1), (2, 0), (1, 1), (3, 1), (1, 0), (3, 0), (0, 1)]
NT = (((1,), (1,)), ((), ()))


def dot(a, b):
    return jnp.dot(a, b, preferred_element_type=F32)


def dot_nt(a, b):
    return lax.dot_general(a, b, NT, preferred_element_type=F32)


def precise(a, b):
    return jnp.dot(a, b, preferred_element_type=F32, precision=lax.Precision.HIGHEST)


def precise_nt(a, b):
    return lax.dot_general(
        a, b, NT, preferred_element_type=F32, precision=lax.Precision.HIGHEST
    )


class Place:
    def __init__(self):
        m = lax.axis_index("mesh")
        t = lax.axis_index("tensor")
        self.zl, self.y, self.c = lax.div(m, 8), lax.rem(lax.div(m, 2), 4), lax.rem(m, 2)
        self.zh, self.x, self.t = lax.div(t, 4), lax.rem(t, 4), t
        self.m = m
        self.g = self.y * 2 + self.c
        x, c = self.x, self.c
        self.xp = (1 - c) * (x + 1 - 2 * lax.rem(x, 2)) + c * (3 - x)
        self.xq = c * (x + 1 - 2 * lax.rem(x, 2)) + (1 - c) * (3 - x)
        self.zp = 1 - self.zh
        self.tq = self.zh * 4 + self.xq

    def peer(self, dy, dc):
        yt, ct = lax.rem(self.y + dy, 4), lax.rem(self.c + dc, 2)
        yf = lax.rem(self.y + 4 - dy, 4)
        to = (self.zl * 8 + yt * 2 + ct, self.t)
        return to, yt * 2 + ct, yf * 2 + ct

    def plane(self, d):
        zt, zf = lax.rem(self.zl + d, 4), lax.rem(self.zl + 4 - d, 4)
        return (zt * 8 + self.g, self.t), zf

    def sibling(self):
        return (self.zl * 8 + self.y * 2 + 1 - self.c, self.t)

    def across(self, x_side, z_side):
        x = self.xp if x_side else self.x
        z = self.zp if z_side else self.zh
        return (self.m, z * 4 + x)

    def other_pair(self):
        return (self.m, self.tq)


class Sends:
    def __init__(self):
        self.all = []

    def start(self, src, dst, send_sem, recv_sem, device):
        copy = pltpu.make_async_remote_copy(
            src_ref=src,
            dst_ref=dst,
            send_sem=send_sem,
            recv_sem=recv_sem,
            device_id=device,
            device_id_type=MESH,
        )
        copy.start()
        self.all.append(copy)
        return copy

    def finish(self):
        for copy in self.all:
            copy.wait_send()
        self.all = []


class AllReduce:
    def __init__(self, place, sends, src, rbuf, zbuf, full, ss, rs):
        self.p, self.sends = place, sends
        self.src, self.rbuf, self.zbuf, self.full = src, rbuf, zbuf, full
        self.ss, self.rs = ss, rs

    def arrived(self, dst, i):
        pltpu.make_async_remote_copy(
            src_ref=dst,
            dst_ref=dst,
            send_sem=self.ss.at[i],
            recv_sem=self.rs.at[i],
            device_id=self.p.sibling(),
            device_id_type=MESH,
        ).wait_recv()

    def step1(self):
        for i, (dy, dc) in enumerate(PEERS):
            to, j, _ = self.p.peer(dy, dc)
            self.sends.start(self.src.at[j], self.rbuf.at[i], self.ss.at[i], self.rs.at[i], to)

    def step2(self):
        for i in range(7):
            self.arrived(self.rbuf.at[i], i)
        total = self.src[self.p.g].astype(F32)
        for i in range(7):
            total += self.rbuf[i].astype(F32)
        zl = self.p.zl
        self.zbuf[zl] = total.astype(self.zbuf.dtype)
        for d in range(1, 4):
            to, _ = self.p.plane(d)
            i = 6 + d
            self.sends.start(self.zbuf.at[zl], self.zbuf.at[zl], self.ss.at[i], self.rs.at[i], to)

    def step3(self):
        for d in range(1, 4):
            _, zf = self.p.plane(d)
            self.arrived(self.zbuf.at[zf], 6 + d)
        total = self.zbuf[0].astype(F32)
        for i in range(1, 4):
            total += self.zbuf[i].astype(F32)
        g = self.p.g
        self.full[g] = total.astype(self.full.dtype)
        for i, (dy, dc) in enumerate(PEERS):
            to, _, _ = self.p.peer(dy, dc)
            k = 10 + i
            self.sends.start(self.full.at[g], self.full.at[g], self.ss.at[k], self.rs.at[k], to)

    def step4(self):
        for i, (dy, dc) in enumerate(PEERS):
            _, _, j = self.p.peer(dy, dc)
            self.arrived(self.full.at[j], 10 + i)


def attention(ar_full, w3, tok_w, on_attended):
    flat = ar_full[...].reshape(SL, 384)
    totals = jnp.sum(flat[:, 256:384], axis=1, keepdims=True)
    denom = totals + 1e-05
    tokens = flat[:, 0:128] / denom
    d_out = flat[:, 128:256]
    scale = 1.0 / (DIM**0.5)
    qkv = precise(tokens, w3[...])
    q, k, v = qkv[:, 0:128], qkv[:, 128:256], qkv[:, 256:384]
    s = precise_nt(q, k) * scale
    st = precise_nt(k, q) * scale
    dp = precise_nt(d_out, v)
    dpt = precise_nt(v, d_out)
    e = jnp.exp(s - jnp.max(s, axis=1, keepdims=True))
    p = e / jnp.sum(e, axis=1, keepdims=True)
    et = jnp.exp(st - jnp.max(st, axis=0, keepdims=True))
    pt = et / jnp.sum(et, axis=0, keepdims=True)
    on_attended(precise(p, v).astype(BF16))
    ds = p * (dp - jnp.sum(p * dp, axis=1, keepdims=True)) * scale
    dst = pt * (dpt - jnp.sum(pt * dpt, axis=0, keepdims=True)) * scale
    dv = precise(pt, d_out)
    dq = precise(ds, k)
    dk = precise(dst, q)
    tok_w[:, 0:128] = dq
    tok_w[:, 128:256] = dk
    tok_w[:, 256:384] = dv
    grad_tokens = precise_nt(tok_w[...], w3[...])
    grad_sums = (grad_tokens / denom).astype(BF16)
    prod = grad_tokens * tokens
    col = -jnp.sum(prod, axis=1, keepdims=True) / denom
    return grad_sums, col


def main_kernel(
    cells_h, cot_h, counts, fx_h, xw_h, swt_h, qw_h, kw_h, vw_h, ow_h,
    out_h, fxg_h, xg_h, sg_h, og_h,
    cells, cot, w, wo, swt, w3, fu, pf, st, xs, xr, own, outb, fxg, xg, sg, og, mt, tokw,
    acc, accb, ag, gt, at1, at2,
    a1r, a1z, a1f, a2s, a2r, a2z, a2f, a3s, a3r, a3z, a3f,
    lsem, csem, tsem, osem, wss, wrs, gss, grs, xss, xrs,
    s1, r1, s2, r2, s3, r3,
):
    p = Place()
    sends = Sends()
    last = Sends()

    def load(src, dst, sem):
        copy = pltpu.make_async_copy(src, dst, sem)
        copy.start()
        return copy

    l_fx = load(fx_h, w.at[:, 0:128], lsem.at[0])
    l_xw = load(xw_h, w.at[:, 128:256], lsem.at[1])
    l_sw = load(swt_h.at[0], swt.at[0], lsem.at[2])
    l_ow = load(ow_h, wo.at[0], lsem.at[3])
    l_cells, l_cot = [], []
    for r in range(NCHUNK):
        rows = pl.ds(r * CHUNK, CHUNK)
        l_cells.append(load(cells_h.at[rows], cells.at[rows], csem.at[r]))
        l_cot.append(load(cot_h.at[rows], cot.at[rows], tsem.at[r]))
    l_q = load(qw_h.at[0], w3.at[:, 0:128], lsem.at[4])
    l_k = load(kw_h.at[0], w3.at[:, 128:256], lsem.at[5])
    l_v = load(vw_h.at[0], w3.at[:, 256:384], lsem.at[6])

    barrier = pltpu.get_barrier_semaphore()
    friends = [p.peer(dy, dc)[0] for dy, dc in PEERS]
    friends += [p.plane(d)[0] for d in range(1, 4)]
    friends += [p.across(0, 1), p.across(1, 0), p.across(1, 1), p.other_pair()]
    for device in friends:
        pl.semaphore_signal(barrier, inc=1, device_id=device, device_id_type=MESH)

    c, y = p.c, p.y
    x_pair, z_pair = p.across(1, 0), p.across(0, 1)

    def start(i, src, dst, device):
        sends.start(src, dst, wss.at[i], wrs.at[i], device)

    def arrived(dst, ssem, rsem):
        pltpu.make_async_remote_copy(
            src_ref=dst, dst_ref=dst, send_sem=ssem, recv_sem=rsem,
            device_id=p.sibling(), device_id_type=MESH,
        ).wait_recv()

    def landed(i, dst):
        arrived(dst, wss.at[i], wrs.at[i])

    def w_part(core, quarter, lanes):
        rows = pl.ds(pl.multiple_of(core * 512 + quarter * 128, 128), 128)
        return w.at[rows, lanes]

    def w_half(core, lanes):
        return w.at[pl.ds(pl.multiple_of(core * 512, 512), 512), lanes]

    def wo_part(slot, core, quarter):
        return wo.at[slot, pl.ds(pl.multiple_of(core * 64 + quarter * 16, 16), 16), :]

    def wo_half(slot, core):
        return wo.at[slot, pl.ds(pl.multiple_of(core * 64, 64), 64), :]

    FX0, FX1, FX2 = slice(0, 256), slice(256, 512), slice(512, 768)
    F2, X2, X3, F3 = slice(512, 640), slice(640, 768), slice(768, 896), slice(896, 1024)

    def spread_w():
        landed(0, w_part(c, y, FX2))
        for d in range(1, 4):
            start(3 + d, w_part(c, y, FX2), w_part(c, y, FX2), p.peer(d, 0)[0])
        start(12, w_part(c, y, X2), w_part(c, y, X3), x_pair)
        start(14, w_part(c, y, F2), w_part(c, y, F3), x_pair)

    def spread_wo():
        landed(1, wo_part(2, c, y))
        for d in range(1, 4):
            start(6 + d, wo_part(2, c, y), wo_part(2, c, y), p.peer(d, 0)[0])
        start(15, wo_part(2, c, y), wo_part(3, c, y), x_pair)

    quarters = [(d, lax.rem(y + 4 - d, 4)) for d in range(1, 4)]

    def gather_w():
        for d in range(1, 4):
            landed(3 + d, w_part(c, lax.rem(y + 4 - d, 4), FX2))
        start(10, w_half(c, FX2), w_half(c, FX2), p.sibling())
        for d, q in quarters:
            start(17 + d, w_part(c, q, X2), w_part(c, q, X3), x_pair)

    def gather_wo():
        for d in range(1, 4):
            landed(6 + d, wo_part(2, c, lax.rem(y + 4 - d, 4)))
        start(11, wo_half(2, c), wo_half(2, c), p.sibling())

    def pass_on():
        landed(10, w_half(1 - c, FX2))
        start(13, w_half(1 - c, X2), w_half(1 - c, X3), x_pair)
        for d, q in quarters:
            start(20 + d, w_part(c, q, F2), w_part(c, q, F3), x_pair)
            start(23 + d, wo_part(2, c, q), wo_part(3, c, q), x_pair)

    def pass_on_rest():
        landed(11, wo_half(2, 1 - c))
        start(16, w_half(1 - c, F2), w_half(1 - c, F3), x_pair)
        start(17, wo_half(2, 1 - c), wo_half(3, 1 - c), x_pair)

    count = counts[0]

    def big_rows(r):
        return pl.ds(pl.multiple_of(r * BIG, BIG), BIG)

    def softmax(k, first, size, mixed):
        rows = pl.ds(first, size)
        logits = dot_nt(swt[k], mixed)
        e = jnp.exp(logits - jnp.max(logits, axis=0, keepdims=True))
        lane = lax.broadcasted_iota(jnp.int32, (1, size), 1) + first
        norm = jnp.where(lane < count, 1.0 / jnp.sum(e, axis=0, keepdims=True), 0.0)
        prob = e * norm
        pf[k, :, rows] = prob
        prob_b = prob.astype(BF16)
        st[k * 128 : k * 128 + 64, rows] = prob_b
        return prob, prob_b

    acc[...] = jnp.zeros_like(acc)

    def own_rows(first, size):
        rows = pl.ds(first, size)
        parts = range(first // CHUNK, (first + size) // CHUNK)
        for r in parts:
            l_cells[r].wait()
        xf = dot(cells[rows, :], w[:, FX0]).astype(BF16)
        fu[0, rows, 0:128] = xf[:, 0:128]
        prob, prob_b = softmax(0, first, size, xf[:, 128:256])
        for r in parts:
            l_cot[r].wait()
        fu[0, rows, 128:256] = dot_nt(cot[rows, :], wo[0]).astype(BF16)
        acc[:, 0:256] += dot(prob_b, fu[0, rows, :])
        tot = acc[:, 256:384]
        for j in range(size // 128):
            tot += prob[:, j * 128 : j * 128 + 128]
        acc[:, 256:384] = tot

    l_fx.wait()
    l_xw.wait()
    l_sw.wait()
    l_ow.wait()
    own_rows(0, CHUNK)
    pl.semaphore_wait(barrier, len(friends))
    start(0, w_part(c, y, FX0), w_part(c, y, FX2), z_pair)
    start(1, wo_part(0, c, y), wo_part(2, c, y), z_pair)
    sends.start(swt.at[0], swt.at[2], gss.at[0], grs.at[0], z_pair)
    start(2, w.at[:, FX0], w.at[:, FX1], x_pair)
    sends.start(swt.at[0], swt.at[1], gss.at[1], grs.at[1], x_pair)
    start(3, wo.at[0], wo.at[1], x_pair)
    own_rows(CHUNK, ROWS - CHUNK)
    accb[...] = acc[...].reshape(8, 8, 384)
    ar1 = AllReduce(p, sends, accb, a1r, a1z, a1f, s1, r1)
    ar2 = AllReduce(p, sends, a2s, a2r, a2z, a2f, s2, r2)
    ar3 = AllReduce(p, sends, a3s, a3r, a3z, a3f, s3, r3)
    ar1.step1()

    def products(lhs_row, rhs, dst, at):
        def body(j, _):
            cols = pl.ds(pl.multiple_of(j * 512, 512), 512)
            out = dot(st[lhs_row : lhs_row + 64, :], rhs[:, cols]).astype(BF16)
            for i in range(4):
                dst[4 * j + i, :, at : at + 128] = out[:, i * 128 : i * 128 + 128]
            return 0

        lax.fori_loop(0, 2, body, 0)

    products(0, cells, a2s, 0)
    spread_w()
    ar1.step2()
    spread_wo()
    products(0, cot, a2s, 128)
    arrived(swt.at[2], gss.at[0], grs.at[0])
    sends.start(swt.at[2], swt.at[3], gss.at[2], grs.at[2], x_pair)
    def pair_body(r, _):
        rows = big_rows(r)
        xf = dot(cells[rows, :], w[:, FX1]).astype(BF16)
        fu[1, rows, 0:128] = xf[:, 0:128]
        softmax(1, pl.multiple_of(r * BIG, BIG), BIG, xf[:, 128:256])
        fu[1, rows, 128:256] = dot_nt(cot[rows, :], wo[1]).astype(BF16)
        return 0

    ar1.step3()
    arrived(swt.at[1], gss.at[1], grs.at[1])
    landed(2, w.at[:, FX1])
    landed(3, wo.at[1])
    pair_body(0, 0)
    gather_w()
    gather_wo()
    pair_body(1, 0)
    pass_on()
    l_q.wait()
    l_k.wait()
    l_v.wait()
    ar1.step4()
    readers = ((3, p.across(1, 1)), (2, z_pair), (1, x_pair))
    GS, ATT = slice(0, 128), slice(128, 256)

    def on_attended(att):
        ag[0, :, ATT] = att
        for slot, device in readers:
            i = 8 + slot
            sends.start(ag.at[0, :, ATT], ag.at[slot, :, ATT], gss.at[i], grs.at[i], device)

    gsum, col0 = attention(a1f, w3, tokw, on_attended)
    ag[0, :, GS] = gsum
    eye = (
        lax.broadcasted_iota(jnp.int32, (SL, SL), 0)
        == lax.broadcasted_iota(jnp.int32, (SL, SL), 1)
    )
    gt[0] = jnp.broadcast_to(jnp.sum(jnp.where(eye, col0, 0.0), axis=0, keepdims=True), (8, SL))
    for slot, device in readers:
        i = 1 + 2 * slot
        sends.start(ag.at[0, :, GS], ag.at[slot, :, GS], gss.at[i], grs.at[i], device)
        sends.start(gt.at[0], gt.at[slot], gss.at[i + 1], grs.at[i + 1], device)
    ar2.step1()
    pass_on_rest()

    def vjp(k, rows, gp):
        prob = pf[k, :, rows]
        mean = jnp.sum(prob * gp, axis=0, keepdims=True)
        st[k * 128 + 64 : k * 128 + 128, rows] = (prob * (gp - mean)).astype(BF16)

    def near_vjp(k, col):
        def body(r, _):
            rows = big_rows(r)
            vjp(k, rows, dot_nt(ag[k], fu[k, rows, :]) + col)
            return 0

        lax.fori_loop(0, NBIG, body, 0)

    def column(k):
        return jnp.sum(jnp.where(eye, gt[k][0:1, :], 0.0), axis=1, keepdims=True)

    near_vjp(0, col0)
    products(64, cells, a3s, 0)
    ar3.step1()
    arrived(swt.at[3], gss.at[2], grs.at[2])
    landed(12, w_part(c, y, X3))
    for d, q in quarters:
        landed(17 + d, w_part(c, q, X3))
    landed(13, w_half(1 - c, X3))

    def far_body(r, _):
        mixed = dot(cells[big_rows(r), :], w[:, 640:896]).astype(BF16)
        first = pl.multiple_of(r * BIG, BIG)
        softmax(2, first, BIG, mixed[:, 0:128])
        softmax(3, first, BIG, mixed[:, 128:256])
        return 0

    lax.fori_loop(0, NBIG, far_body, 0)
    ar2.step2()

    f_at = (0, 256, 512, 896)
    x_at = (128, 384, 640, 768)
    col_rows = [pl.ds(pl.multiple_of(t * 128, 128), 128) for t in (p.tq, p.t)]

    def fixed_columns(k):
        for i, rows in enumerate(col_rows):
            mt[i, :, k * 128 + 64 : k * 128 + 128] = dot_nt(
                w[rows, x_at[k] : x_at[k] + 128], swt[k]
            ).astype(BF16)

    def sum_columns(k):
        for i, rows in enumerate(col_rows):
            mt[i, :, k * 128 : k * 128 + 64] = dot_nt(
                w[rows, f_at[k] : f_at[k] + 128], ag[k, :, 0:128]
            ).astype(BF16)

    def attended_from(k):
        arrived(ag.at[k, :, ATT], gss.at[8 + k], grs.at[8 + k])

    def gradients_from(k):
        i = 1 + 2 * k
        arrived(ag.at[k, :, GS], gss.at[i], grs.at[i])
        arrived(gt.at[k], gss.at[i + 1], grs.at[i + 1])

    def centred(k, lanes):
        full = ag[k, :, lanes].astype(F32)
        return (full - jnp.mean(full, axis=0, keepdims=True)).astype(BF16)

    def fold_rows(k):
        return slice((k - 2) * 64, (k - 1) * 64)

    for k in range(4):
        fixed_columns(k)
    sum_columns(0)
    ar3.step2()
    attended_from(1)
    gradients_from(1)
    near_vjp(1, column(1))
    sum_columns(1)
    landed(14, w_part(c, y, F3))
    landed(15, wo_part(3, c, y))
    for d, q in quarters:
        landed(20 + d, w_part(c, q, F3))
        landed(23 + d, wo_part(3, c, q))
    landed(16, w_half(1 - c, F3))
    landed(17, wo_half(3, 1 - c))
    attended_from(2)
    attended_from(3)
    for k in (2, 3):
        at2[fold_rows(k), :] = dot(centred(k, ATT), wo[k]).astype(BF16)
    gradients_from(2)
    gradients_from(3)
    for k in (2, 3):
        lanes = slice(f_at[k], f_at[k] + 128)
        at1[fold_rows(k), :] = dot_nt(centred(k, GS), w[:, lanes]).astype(BF16)
    for k in (2, 3):
        sum_columns(k)
    gcol = [column(k) for k in (2, 3)]
    for r in range(NLATE):
        rows = pl.ds(EDGES[r], EDGES[r + 1] - EDGES[r])
        gp = dot_nt(at1[...], cells[rows, :]) + dot_nt(at2[...], cot[rows, :])
        for k in (2, 3):
            vjp(k, rows, gp[(k - 2) * 64 : (k - 1) * 64, :] + gcol[k - 2])
        xs[:, rows] = dot(mt[0], st[:, rows]).astype(BF16)
        part = slice(EDGES[r], EDGES[r + 1])
        last.start(xs.at[:, part], xr.at[:, part], xss.at[r], xrs.at[r], p.other_pair())
        if r == 1:
            ar2.step3()
        if r == 2:
            ar3.step3()
    for r in range(NCHUNK):
        rows = pl.ds(r * CHUNK, CHUNK)
        own[:, rows] = dot(mt[1], st[:, rows])
    tn = (((0,), (0,)), ((), ()))
    outs = []
    ar2.step4()
    gs = ag[0, :, 0:128]
    att_t = ag[0, :, 128:256].astype(F32).T.astype(BF16)
    for j in range(8):
        cols = slice(j * 128, j * 128 + 128)
        fxg[cols, :] = lax.dot_general(a2f[j, :, 0:128], gs, tn, preferred_element_type=F32)
        og[:, cols] = dot(att_t, a2f[j, :, 128:256])
    outs.append(load(fxg, fxg_h, osem.at[0]))
    outs.append(load(og, og_h, osem.at[1]))
    for r in range(NLATE):
        rows = pl.ds(EDGES[r], EDGES[r + 1] - EDGES[r])
        arrived(xr.at[:, slice(EDGES[r], EDGES[r + 1])], xss.at[r], xrs.at[r])
        total = own[:, rows] + xr[:, rows].astype(F32)
        outb[rows, :] = total.T.astype(BF16)
        outs.append(load(outb.at[rows], out_h.at[rows], osem.at[4 + r]))
        if r == 2:
            ar3.step4()
            swt0 = swt[0]
            total = jnp.zeros((SL, DIM), F32)
            for j in range(8):
                cols = slice(j * 128, j * 128 + 128)
                xg[cols, :] = lax.dot_general(a3f[j], swt0, tn, preferred_element_type=F32)
                total += dot(a3f[j], w[cols, 128:256])
            sg[0] = total
            outs.append(load(xg, xg_h, osem.at[2]))
            outs.append(load(sg, sg_h, osem.at[3]))
            sends.finish()
    for copy in outs:
        copy.wait()
    last.finish()


def finish_kernel(*refs):
    src, dst, held, sem = refs[0:5], refs[5:10], refs[10:15], refs[15]
    inward = [pltpu.make_async_copy(src[i], held[i], sem.at[i]) for i in range(5)]
    outward = [pltpu.make_async_copy(held[i], dst[i], sem.at[5 + i]) for i in range(5)]
    for copy in inward:
        copy.start()
    for i in range(5):
        inward[i].wait()
        outward[i].start()
    for copy in outward:
        copy.wait()


def shards(cells, cot, counts, fx_w, x_w, s_w, q_w, k_w, v_w, o_w):
    hbm = pl.BlockSpec(memory_space=pl.ANY)
    sds = jax.ShapeDtypeStruct
    dma = pltpu.SemaphoreType.DMA
    V = pltpu.VMEM
    swt = jnp.swapaxes(s_w, 1, 2)
    limit = 60 * 1024 * 1024
    shapes = (
        sds((ROWS, DIM), BF16),
        sds((WIDTH, DIM), F32),
        sds((WIDTH, DIM), F32),
        sds((1, SL, DIM), F32),
        sds((DIM, WIDTH), F32),
    )
    held = [V(a.shape, a.dtype) for a in shapes]
    outs = pl.pallas_call(
        main_kernel,
        name="layer",
        out_shape=shapes,
        in_specs=[hbm, hbm, pl.BlockSpec(memory_space=pltpu.SMEM)] + [hbm] * 7,
        out_specs=[hbm] * 5,
        scratch_shapes=[
            V((ROWS, WIDTH), BF16),
            V((ROWS, WIDTH), BF16),
            V((WIDTH, 1024), BF16),
            V((4, DIM, WIDTH), BF16),
            V((4, SL, 128), BF16),
            V((DIM, 384), F32),
            V((2, ROWS, 256), BF16),
            V((4, SL, ROWS), F32),
            V((512, ROWS), BF16),
            V((DIM, ROWS), BF16),
            V((DIM, ROWS), BF16),
            V((DIM, ROWS), F32),
            *held,
            V((2, DIM, 512), BF16),
            V((SL, 384), F32),
            V((SL, 384), F32),
            V((8, 8, 384), F32),
            V((4, SL, 256), BF16),
            V((4, 8, SL), F32),
            V((128, WIDTH), BF16),
            V((128, WIDTH), BF16),
            V((7, 8, 384), F32),
            V((4, 8, 384), F32),
            V((8, 8, 384), F32),
            V((8, SL, 256), BF16),
            V((7, SL, 256), BF16),
            V((4, SL, 256), BF16),
            V((8, SL, 256), BF16),
            V((8, SL, 128), BF16),
            V((7, SL, 128), BF16),
            V((4, SL, 128), BF16),
            V((8, SL, 128), BF16),
            dma((7,)),
            dma((NCHUNK,)),
            dma((NCHUNK,)),
            dma((4 + NLATE,)),
            dma((27,)),
            dma((27,)),
            dma((12,)),
            dma((12,)),
            dma((NLATE,)),
            dma((NLATE,)),
        ]
        + [dma((17,))] * 6,
        compiler_params=pltpu.CompilerParams(
            collective_id=0, has_side_effects=True, vmem_limit_bytes=limit
        ),
    )(cells, cot, counts, fx_w, x_w, swt, q_w, k_w, v_w, o_w)
    outs = pl.pallas_call(
        finish_kernel,
        name="grads",
        out_shape=shapes,
        in_specs=[hbm] * 5,
        out_specs=[hbm] * 5,
        scratch_shapes=[*held, dma((10,))],
        compiler_params=pltpu.CompilerParams(vmem_limit_bytes=limit),
    )(*outs)
    return outs[0], outs[1], outs[2], jnp.swapaxes(outs[3], 1, 2), outs[4]


def solution(mesh):
    in_specs = (
        P("mesh", None),
        P("mesh", None),
        P("mesh"),
        P(None, "tensor"),
        P(None, "tensor"),
        P("tensor", None, None),
        P("tensor", None, None),
        P("tensor", None, None),
        P("tensor", None, None),
        P("tensor", None),
    )
    out_specs = (
        P("mesh", "tensor"),
        P(None, "tensor"),
        P(None, "tensor"),
        P("tensor", None, None),
        P("tensor", None),
    )
    return jax.shard_map(shards, mesh=mesh, in_specs=in_specs, out_specs=out_specs, check_vma=False)
```
